256 devices in a mesh: grp: 16 (over y_lo, x, core), lon: 16 (over y_hi, z).
Axes of the slice: x: 4, y: 4 (y_hi: 2, y_lo: 2; y = y_hi * 2 + y_lo), z: 8, core: 2. Of those that a mesh axis runs over, the one named last changes fastest.
Arguments:
- ensemble: float32 [256, 16, 128, 128], P('grp', None, 'lon'), may hold values from -6 to 6
- courant_east: float32 [16, 128, 128], P(None, 'lon'), may hold values from -0.9 to 0.9
- northward_courant: float32 [16, 128, 128], P(None, 'lon'), may hold values from -0.9 to 0.9
- measured: float32 [64, 1024], P('lon'), may hold values from -6 to 6
- error_variance: float32 [64, 1024], P('lon'), may hold values from 0.25 to 4
- sensor_cell: int32 [64, 1024], P('lon'), may hold values from 0 to 262143, as said below
- sensor_count: int32 [64], P('lon'), may hold values from 256 to 1024, as said below
- perturbation: float32 [256, 64, 1024], P('grp', 'lon'), may hold values from -6 to 6
Outputs:
- analysis: float32 [256, 16, 128, 128], P('grp', None, 'lon')
The draws below stay inside these ranges and needn't reach their ends.
Inputs may be any that keep to these rules, and one draw needn't show every extreme that they name: Region r observes sensor_count[r] cells in its first slots; one region has exactly 1024 observations and another exactly 256. `sensor_cell`: every slot of region r, used or not, names a cell of region r.
All inputs are finite; a program needn't handle non-finite values.
Results may differ from the reference program's by a relative error of at most 0.00027.
Values sent between devices are 32-bit elements; how exact they have to be, the bound alone decides.
A program may use at most 192 MiB of HBM per device.

```python
import math
import jax
import jax.numpy as jnp
from jax import lax

MEMBERS = 256
LEV = 16
LON_DEV = 8
NLON = 128
LAT = 128
REG_DEV = 4
ANALYSIS_REGIONS = 64
BAND = 32
OBSERVATION_SLOTS = 1024
N_LON = 16


mode_total = 48


def draw_sensor_count(key, part):
    key = jax.random.fold_in(key, 1)
    spread = OBSERVATION_SLOTS - OBSERVATION_SLOTS // 4
    key_steps, key_heavy, key_light = jax.random.split(key, 3)
    stepped = jax.random.randint(key_steps, (ANALYSIS_REGIONS,), 0, spread + 1)
    counts = OBSERVATION_SLOTS // 4 + stepped * stepped // spread
    heaviest = jax.random.randint(key_heavy, (), 0, ANALYSIS_REGIONS)
    lightest = (heaviest + 1 + jax.random.randint(key_light, (), 0, ANALYSIS_REGIONS - 1)) % ANALYSIS_REGIONS
    counts = counts.at[heaviest].set(OBSERVATION_SLOTS).at[lightest].set(OBSERVATION_SLOTS // 4)
    return counts.astype(jnp.int32)


def draw_sensor_cell(key, part):
    key = jax.random.fold_in(key, 2)
    key_level, key_column, key_row = jax.random.split(key, 3)
    region = jnp.arange(ANALYSIS_REGIONS, dtype=jnp.int32)[:, None]
    level_pick = jax.random.randint(key_level, (ANALYSIS_REGIONS, OBSERVATION_SLOTS), 0, LEV)
    column_pick = region // REG_DEV * LON_DEV + jax.random.randint(key_column, (ANALYSIS_REGIONS, OBSERVATION_SLOTS), 0, LON_DEV)
    row_pick = region % REG_DEV * BAND + jax.random.randint(key_row, (ANALYSIS_REGIONS, OBSERVATION_SLOTS), 0, BAND)
    return ((level_pick * NLON + column_pick) * LAT + row_pick).astype(jnp.int32)


def smooth_modes(key, total_power, decay_power):
    key_coef, key_level, key_column, key_row, key_phase = jax.random.split(key, 5)
    coefficients = jax.random.normal(key_coef, (MEMBERS, mode_total), jnp.float32)
    level_wave = jax.random.uniform(key_level, (mode_total,), jnp.float32, -1.0, 1.0)
    column_wave = jax.random.uniform(key_column, (mode_total,), jnp.float32, 0.0, 0.75)
    row_wave = jax.random.uniform(key_row, (mode_total,), jnp.float32, -1.5, 1.5)
    phases = jax.random.uniform(key_phase, (mode_total,), jnp.float32, -math.pi, math.pi)
    norm_total = sum(((j + 1.0) ** (-decay_power) for j in range(mode_total)))
    amplitude = jnp.asarray([math.sqrt(2.0 * total_power * (j + 1.0) ** (-decay_power) / norm_total) for j in range(mode_total)], jnp.float32)
    level_grid = lax.broadcasted_iota(jnp.float32, (LEV, NLON, LAT), 0) / LEV
    column_grid = lax.broadcasted_iota(jnp.float32, (LEV, NLON, LAT), 1) / LON_DEV
    row_grid = lax.broadcasted_iota(jnp.float32, (LEV, NLON, LAT), 2) / BAND

    def add_mode(index, field):
        angle = 2.0 * math.pi * (level_wave[index] * level_grid + column_wave[index] * column_grid + row_wave[index] * row_grid) + phases[index]
        member_scale = amplitude[index] * coefficients[:, index]
        return field + member_scale[:, None, None, None] * jnp.cos(angle)[None]
    start_field = jnp.zeros((MEMBERS, LEV, NLON, LAT), jnp.float32)
    return lax.fori_loop(0, mode_total, add_mode, start_field)


def draw_ensemble(key, part):
    key = jax.random.fold_in(key, 3)
    key_noise, key_modes = jax.random.split(key, 2)
    noise = jax.random.normal(key_noise, (MEMBERS, LEV, NLON, LAT), jnp.float32)
    smooth = smooth_modes(key_modes, 0.8, 1.0)
    return jnp.clip(noise + smooth, -6.0, 6.0).astype(jnp.float32)


def level_of(own_key, dims, cuts, low, high):
    factor_of = 1.0
    for position, blocks in cuts:
        draws = jax.random.uniform(jax.random.fold_in(jax.random.fold_in(own_key, 6), position), (blocks,), jnp.float32, low / len(cuts), high / len(cuts))
        factor_of = factor_of * jnp.repeat(jnp.exp(draws), dims[position] // blocks).reshape((-1,) + (1,) * (len(dims) - 1 - position))
    return factor_of


def centred(stream_key, shape, deviation, reach, shards=(), kind=jnp.bfloat16):
    values = deviation * jax.random.normal(stream_key, shape, jnp.float32)
    if shards:
        values = values * level_of(stream_key, shape, shards, -0.22, 0.18)
    return jnp.clip(values, -reach, reach).astype(kind)


def setup_inputs(seed: int = 0) -> dict:
    arg_keys = jax.random.split(jax.random.key(seed), 9)
    return {
        "ensemble": draw_ensemble(jax.random.fold_in(arg_keys[8], 71), 0),
        "courant_east": jnp.clip(jax.random.uniform(arg_keys[1], (LEV, NLON, LAT), jnp.float32, -0.9, 0.9) * level_of(arg_keys[1], (LEV, NLON, LAT), ((1, 16),), -0.4, 0.0), -0.9, 0.9),
        "northward_courant": jnp.clip(jax.random.uniform(arg_keys[2], (LEV, NLON, LAT), jnp.float32, -0.9, 0.9) * level_of(arg_keys[2], (LEV, NLON, LAT), ((1, 16),), -0.4, 0.0), -0.9, 0.9),
        "measured": centred(arg_keys[3], (ANALYSIS_REGIONS, OBSERVATION_SLOTS), 1.0, 6.0, ((0, 16),), jnp.float32),
        "error_variance": jnp.clip(jnp.exp(math.log(4.0) - 2.7725887 * jax.random.uniform(arg_keys[4], (ANALYSIS_REGIONS, OBSERVATION_SLOTS), jnp.float32) ** level_of(arg_keys[4], (ANALYSIS_REGIONS, OBSERVATION_SLOTS), ((0, 16),), -0.2, 0.2)), 0.25, 4.0),
        "sensor_cell": draw_sensor_cell(jax.random.fold_in(arg_keys[8], 71), 0),
        "sensor_count": draw_sensor_count(jax.random.fold_in(arg_keys[8], 71), 0),
        "perturbation": centred(arg_keys[7], (MEMBERS, ANALYSIS_REGIONS, OBSERVATION_SLOTS), 1.0, 6.0, ((0, 16), (1, 16)), jnp.float32),
    }


def cycle_step(state_field, courant):
    eastern = jnp.roll(state_field, -1, axis=2)
    western = jnp.roll(state_field, 1, axis=2)
    return state_field - 0.5 * courant * (eastern - western) + 0.5 * courant * courant * (eastern - 2.0 * state_field + western)

def boundary_step(state_field, courant):
    padded = jnp.pad(state_field, ((0, 0), (0, 0), (0, 0), (1, 1)))
    northern = padded[..., 2:]
    southern = padded[..., :-2]
    return state_field - 0.5 * courant * (northern - southern) + 0.5 * courant * courant * (northern - 2.0 * state_field + southern)

def solve_region(region_items):
    anomaly_rows, innovation_rows, variance_row = region_items
    covariance = jnp.dot(anomaly_rows.T.astype(jnp.float32), anomaly_rows.astype(jnp.float32), precision=lax.Precision.HIGHEST, preferred_element_type=jnp.float32) + jnp.diag(variance_row)
    factor_lower = jnp.linalg.cholesky(covariance)
    solved = jax.scipy.linalg.cho_solve((factor_lower, True), innovation_rows.T)
    return jnp.dot(anomaly_rows.astype(jnp.float32), solved.astype(jnp.float32), precision=lax.Precision.HIGHEST, preferred_element_type=jnp.float32)

def reference(ensemble, courant_east, northward_courant, measured, error_variance, sensor_cell, sensor_count, perturbation):
    half_time_step = cycle_step(ensemble, courant_east)
    prior_state = boundary_step(half_time_step, northward_courant)
    ensemble_members = prior_state.shape[0]
    inflation_scale = 1.0 / math.sqrt(ensemble_members - 1)
    member_deviation = prior_state - lax.optimization_barrier(jnp.sum(prior_state, axis=0)) / ensemble_members
    region_cell_list = sensor_cell.reshape(-1)
    seen_anomaly = jnp.take(member_deviation.reshape(ensemble_members, -1), region_cell_list, axis=1).reshape(ensemble_members, ANALYSIS_REGIONS, OBSERVATION_SLOTS)
    observed_prior = jnp.take(prior_state.reshape(ensemble_members, -1), region_cell_list, axis=1).reshape(ensemble_members, ANALYSIS_REGIONS, OBSERVATION_SLOTS)
    valid = jnp.where(jnp.arange(OBSERVATION_SLOTS, dtype=jnp.int32)[None, :] < sensor_count[:, None], 1, 0).astype(jnp.int32)
    slot_is_valid = valid > 0
    observed = jnp.where(slot_is_valid[None], seen_anomaly * inflation_scale, 0.0)
    observation_misfit = jnp.where(slot_is_valid[None], measured[None] + perturbation - observed_prior, 0.0)
    variance = jnp.where(slot_is_valid, error_variance, 1.0)
    weights = lax.map(solve_region, (jnp.swapaxes(observed, 0, 1), jnp.swapaxes(observation_misfit, 0, 1), variance))
    weight_grid = weights.reshape(N_LON, REG_DEV, ensemble_members, ensemble_members)
    anomaly_grid = member_deviation.reshape(ensemble_members, LEV, N_LON, LON_DEV, REG_DEV, BAND)
    analysis_update = jnp.einsum('sbpm,plsxbc->mlsxbc', weight_grid, anomaly_grid, precision=lax.Precision.HIGHEST)
    return prior_state + inflation_scale * analysis_update.reshape(prior_state.shape)
```

```python
import functools
import math

import jax
import jax.numpy as jnp
from jax import lax
from jax.experimental import pallas as pl
from jax.experimental.pallas import tpu as pltpu
from jax.sharding import PartitionSpec as P

MESH = pl.DeviceIdType.MESH
F32 = jnp.float32
BF16 = jnp.bfloat16
NG = 16
NS = 16
MB = 16
M = 256
LEV = 16
LON = 8
LAT = 128
NB = 4
NQ = 4
NO = 1024
SCALE = 1.0 / math.sqrt(M - 1)
VMEM = pl.BlockSpec(memory_space=pltpu.VMEM)
SMEM = pl.BlockSpec(memory_space=pltpu.SMEM)


def split2(x):
    hi = x.astype(BF16)
    lo = (x - hi.astype(F32)).astype(BF16)
    return hi, lo


def send_kernel(
    ens_ref, ce_ref, cn_ref, pert_ref, cell_ref,
    zr_ref, pt_ref, ft_ref,
    hsrc, hdst, coef, fp, lhs, zb, pb,
    h_send, h_recv, p_send, p_recv, z_send, z_recv, f_send, f_recv,
):
    g = lax.axis_index("grp")
    s = lax.axis_index("lon")
    my_b, my_q = g // NQ, lax.rem(g, NQ)
    east, west = lax.rem(s + 1, NS), lax.rem(s + NS - 1, NS)

    barrier = pltpu.get_barrier_semaphore()
    for i in range(1, NG):
        pl.semaphore_signal(barrier, inc=1, device_id={"grp": lax.rem(g + i, NG)}, device_id_type=MESH)
    for n in (east, west):
        pl.semaphore_signal(barrier, inc=1, device_id={"lon": n}, device_id_type=MESH)

    hsrc[0] = ens_ref[:, :, LON - 1, :]
    hsrc[1] = ens_ref[:, :, 0, :]
    for b in range(NB):
        pb[b] = pert_ref[:, b, :]
    pl.semaphore_wait(barrier, NG - 1 + 2)

    def halo(i, to):
        return pltpu.make_async_remote_copy(
            src_ref=hsrc.at[i], dst_ref=hdst.at[i], send_sem=h_send.at[i], recv_sem=h_recv.at[i],
            device_id={"lon": to}, device_id_type=MESH)

    halo(0, east).start()
    halo(1, west).start()

    def pert_copy(to):
        return pltpu.make_async_remote_copy(
            src_ref=pb.at[to // NQ], dst_ref=pt_ref.at[pl.ds(g * MB, MB)],
            send_sem=p_send.at[to], recv_sem=p_recv.at[g],
            device_id={"grp": to}, device_id_type=MESH)

    def z_copy(to):
        return pltpu.make_async_remote_copy(
            src_ref=zb.at[to // NQ], dst_ref=zr_ref.at[pl.ds(g * MB, MB)],
            send_sem=z_send.at[to], recv_sem=z_recv.at[g],
            device_id={"grp": to}, device_id_type=MESH)

    def f_copy(to):
        return pltpu.make_async_remote_copy(
            src_ref=fp.at[to], dst_ref=ft_ref.at[:, pl.ds(g * MB, MB), :],
            send_sem=f_send.at[to], recv_sem=f_recv.at[g],
            device_id={"grp": to}, device_id_type=MESH)

    @pl.loop(1, NG)
    def _(i):
        pert_copy(lax.rem(g + i, NG)).start()

    pt_ref[pl.ds(g * MB, MB), :] = pb[my_b]

    lane = lax.broadcasted_iota(jnp.int32, (LON, LAT), 1)
    sub = lax.broadcasted_iota(jnp.int32, (LON, LAT), 0)
    for l in range(LEV):
        c = ce_ref[l]
        coef[0, l] = 1.0 - c * c
        coef[1, l] = 0.5 * (c * c - c)
        coef[2, l] = 0.5 * (c * c + c)
        c = cn_ref[l]
        coef[3, l] = 1.0 - c * c
        coef[4, l] = jnp.where(lane == LAT - 1, 0.0, 0.5 * (c * c - c))
        coef[5, l] = jnp.where(lane == 0, 0.0, 0.5 * (c * c + c))

    halo(0, east).wait()
    halo(1, west).wait()

    block = lane // 32
    for q in range(NQ):
        @pl.loop(0, MB)
        def _(m):
            tiles = []
            for k in range(4):
                l = 4 * q + k
                e = ens_ref[m, l]
                w_edge = jnp.broadcast_to(hdst[0, m, pl.ds(l, 1), :], (LON, LAT))
                e_edge = jnp.broadcast_to(hdst[1, m, pl.ds(l, 1), :], (LON, LAT))
                ww = jnp.where(sub == 0, w_edge, pltpu.roll(e, 1, 0))
                ee = jnp.where(sub == LON - 1, e_edge, pltpu.roll(e, LON - 1, 0))
                half = coef[0, l] * e + coef[1, l] * ee + coef[2, l] * ww
                tiles.append(coef[3, l] * half + coef[4, l] * pltpu.roll(half, LAT - 1, 1)
                             + coef[5, l] * pltpu.roll(half, 1, 1))
            for b in range(NB):
                out = None
                for k in range(4):
                    shift = (32 * (k - b)) % LAT
                    t = pltpu.roll(tiles[k], shift, 1) if shift else tiles[k]
                    out = t if out is None else jnp.where(block == k, t, out)
                for x in range(LON):
                    fp[b * NQ + q, x, pl.ds(m, 1), :] = out[x:x + 1]

    @pl.loop(1, NG)
    def _(i):
        f_copy(lax.rem(g + i, NG)).start()

    ft_ref[:, pl.ds(g * MB, MB), :] = fp[g]

    rows = lax.broadcasted_iota(jnp.int32, (LAT, NO), 0)

    @pl.loop(0, NB)
    def _(i):
        b = lax.rem(my_b + i, NB)
        cell = cell_ref[pl.ds(b, 1), :]
        level = cell // (NS * LON * LAT)
        low = (level % 4) * 32 + cell % 32
        high = (level // 4) * LON + (cell // LAT) % LON
        pick = jnp.where(rows == low, 1.0, 0.0).astype(BF16)
        for o in range(0, NO, 256):
            acc = jnp.zeros((MB, 256), F32)
            hi_o = jnp.broadcast_to(high[:, o:o + 256], (MB, 256))
            pk = pick[:, o:o + 256]
            for q in range(NQ):
                f = fp[b * NQ + q].reshape(LON * MB, LAT)
                h0 = f.astype(BF16)
                r = f - h0.astype(F32)
                h1 = r.astype(BF16)
                h2 = (r - h1.astype(F32)).astype(BF16)
                t = jnp.dot(jnp.concatenate([h0, h1, h2], axis=1),
                            jnp.concatenate([pk, pk, pk], axis=0), preferred_element_type=F32)
                for x in range(LON):
                    acc = acc + jnp.where(hi_o == q * LON + x, t[x * MB:(x + 1) * MB], 0.0)
            zb[b, :, o:o + 256] = acc

        @pl.loop(0, NQ)
        def _(j):
            to = b * NQ + lax.rem(my_q + j, NQ)

            @pl.when(to != g)
            def _():
                z_copy(to).start()

    zr_ref[pl.ds(g * MB, MB), :] = zb[my_b]

    @pl.loop(1, NG)
    def _(i):
        to = lax.rem(g + i, NG)
        src = lax.rem(g + NG - i, NG)
        for make, ref, sem in ((pert_copy, pt_ref, p_recv), (z_copy, zr_ref, z_recv)):
            make(to).wait_send()
            pltpu.make_async_remote_copy(
                src_ref=pb.at[0], dst_ref=ref.at[pl.ds(src * MB, MB)],
                send_sem=p_send.at[to], recv_sem=sem.at[src],
                device_id={"grp": to}, device_id_type=MESH).wait_recv()
        f_copy(to).wait_send()
        pltpu.make_async_remote_copy(
            src_ref=fp.at[0], dst_ref=ft_ref.at[:, pl.ds(src * MB, MB), :],
            send_sem=f_send.at[to], recv_sem=f_recv.at[src],
            device_id={"grp": to}, device_id_type=MESH).wait_recv()


def dot(a, b, dims=((1,), (0,))):
    return lax.dot_general(a, b, (dims, ((), ())), precision=lax.Precision.HIGHEST, preferred_element_type=F32)


def solve_kernel(zr_ref, pt_ref, ft_ref, meas_ref, var_ref, count_ref, an_ref, mat, inv, yt):
    b = lax.axis_index("grp") // NQ
    zr = zr_ref[...]
    mean = jnp.sum(zr, axis=0, keepdims=True) * (1.0 / M)
    slot = lax.broadcasted_iota(jnp.int32, (1, NO), 1)
    weight = jnp.where(slot < count_ref[b], 1.0 / var_ref[pl.ds(b, 1), :], 0.0)
    z = (zr - mean) * SCALE
    zw = z * weight
    d = (meas_ref[pl.ds(b, 1), :] + pt_ref[...]) - zr
    eye = jnp.where(lax.broadcasted_iota(jnp.int32, (M, M), 0) == lax.broadcasted_iota(jnp.int32, (M, M), 1), 1.0, 0.0)
    spread = dot(zw, z, ((1,), (1,)))
    rhs_t = dot(d, zw, ((1,), (1,)))
    bound = jnp.sqrt(jnp.sum(spread * spread)) * 1.0001 + 1.0
    mat[...] = spread + eye

    low = 1.0 / bound
    k = 4.0 / ((1.0 + low) * (1.0 + low))
    inv[...] = (k * low) * ((1.0 + low) * eye - low * mat[...])

    def go_on(low):
        return low < 0.97

    def step(low):
        k = 4.0 / ((1.0 + low) * (1.0 + low))
        x = inv[...]
        r = (1.0 + low) * eye - dot(mat[...], x)
        inv[...] = k * dot(x, r)
        return k * low

    low = lax.while_loop(go_on, step, k * low)
    x = inv[...] * (2.0 / (1.0 + low))
    y = dot(rhs_t, x)
    for _ in range(2):
        y = y + dot(rhs_t - dot(y, mat[...]), x)
    y = y * SCALE
    y0, y1 = split2(y)
    lhs = jnp.concatenate([y0, y0, y1], axis=1)
    for x in range(0, LON, 2):
        f = jnp.concatenate([ft_ref[x], ft_ref[x + 1]], axis=1)
        a = f - jnp.sum(f, axis=0, keepdims=True) * (1.0 / M)
        a0, a1 = split2(a)
        u = f + jnp.dot(lhs, jnp.concatenate([a0, a1, a0], axis=0), preferred_element_type=F32)
        an_ref[x] = u[:, :LAT]
        an_ref[x + 1] = u[:, LAT:]


def return_kernel(an_ref, out_ref, rb, send, recv):
    g = lax.axis_index("grp")
    barrier = pltpu.get_barrier_semaphore()
    for i in range(1, NG):
        pl.semaphore_signal(barrier, inc=1, device_id={"grp": lax.rem(g + i, NG)}, device_id_type=MESH)
    pl.semaphore_wait(barrier, NG - 1)

    def copy(to):
        return pltpu.make_async_remote_copy(
            src_ref=an_ref.at[:, pl.ds(to * MB, MB), :], dst_ref=rb.at[g],
            send_sem=send.at[to], recv_sem=recv.at[g],
            device_id={"grp": to}, device_id_type=MESH)

    @pl.loop(1, NG)
    def _(i):
        copy(lax.rem(g + i, NG)).start()

    rb[g] = an_ref[:, pl.ds(g * MB, MB), :]

    @pl.loop(1, NG)
    def _(i):
        to = lax.rem(g + i, NG)
        src = lax.rem(g + NG - i, NG)
        copy(to).wait_send()
        pltpu.make_async_remote_copy(
            src_ref=rb.at[g], dst_ref=rb.at[src], send_sem=send.at[to], recv_sem=recv.at[src],
            device_id={"grp": to}, device_id_type=MESH).wait_recv()

    block = lax.broadcasted_iota(jnp.int32, (LON, LAT), 1) // 32
    for q in range(NQ):
        @pl.loop(0, MB)
        def _(m):
            tiles = []
            for b in range(NB):
                tiles.append(jnp.concatenate([rb[b * NQ + q, x, pl.ds(m, 1), :] for x in range(LON)], axis=0))
            for k in range(4):
                out = None
                for b in range(NB):
                    shift = (32 * (b - k)) % LAT
                    t = pltpu.roll(tiles[b], shift, 1) if shift else tiles[b]
                    out = t if out is None else jnp.where(block == b, t, out)
                out_ref[m, 4 * q + k] = out


def on_device(ensemble, courant_east, northward_courant, measured, error_variance, sensor_cell, sensor_count, perturbation):
    dma = pltpu.SemaphoreType.DMA
    zr, pt, ft = pl.pallas_call(
        send_kernel,
        out_shape=(
            jax.ShapeDtypeStruct((M, NO), F32),
            jax.ShapeDtypeStruct((M, NO), F32),
            jax.ShapeDtypeStruct((LON, M, LAT), F32),
        ),
        in_specs=[VMEM] * 5,
        out_specs=(VMEM,) * 3,
        scratch_shapes=[
            pltpu.VMEM((2, MB, LEV, LAT), F32),
            pltpu.VMEM((2, MB, LEV, LAT), F32),
            pltpu.VMEM((6, LEV, LON, LAT), F32),
            pltpu.VMEM((NG, LON, MB, LAT), F32),
            pltpu.VMEM((LON * MB, 3 * LAT), BF16),
            pltpu.VMEM((NB, MB, NO), F32),
            pltpu.VMEM((NB, MB, NO), F32),
            dma((2,)), dma((2,)), dma((NG,)), dma((NG,)), dma((NG,)), dma((NG,)), dma((NG,)), dma((NG,)),
        ],
        compiler_params=pltpu.CompilerParams(collective_id=0, has_side_effects=True, vmem_limit_bytes=48 << 20),
    )(ensemble, courant_east, northward_courant, perturbation, sensor_cell)
    an = pl.pallas_call(
        solve_kernel,
        out_shape=jax.ShapeDtypeStruct((LON, M, LAT), F32),
        in_specs=[VMEM] * 5 + [SMEM],
        out_specs=VMEM,
        scratch_shapes=[pltpu.VMEM((M, M), F32), pltpu.VMEM((M, M), F32), pltpu.VMEM((M, M), F32)],
        compiler_params=pltpu.CompilerParams(vmem_limit_bytes=48 << 20),
    )(zr, pt, ft, measured, error_variance, sensor_count)
    return pl.pallas_call(
        return_kernel,
        out_shape=jax.ShapeDtypeStruct((MB, LEV, LON, LAT), F32),
        in_specs=[VMEM],
        out_specs=VMEM,
        scratch_shapes=[pltpu.VMEM((NG, LON, MB, LAT), F32), dma((NG,)), dma((NG,))],
        compiler_params=pltpu.CompilerParams(collective_id=1, has_side_effects=True, vmem_limit_bytes=48 << 20),
    )(an)


def solution(mesh):
    return jax.shard_map(
        on_device,
        mesh=mesh,
        in_specs=(
            P("grp", None, "lon", None),
            P(None, "lon", None),
            P(None, "lon", None),
            P("lon", None),
            P("lon", None),
            P("lon", None),
            P("lon"),
            P("grp", "lon", None),
        ),
        out_specs=P("grp", None, "lon", None),
        check_vma=False,
    )
```

```python
import functools
import math

import jax
import jax.numpy as jnp
from jax import lax
from jax.experimental import pallas as pl
from jax.experimental.pallas import tpu as pltpu
from jax.sharding import PartitionSpec as P

MESH = pl.DeviceIdType.MESH
F32 = jnp.float32
BF16 = jnp.bfloat16
NG = 16
NS = 16
MB = 16
M = 256
LEV = 16
LON = 8
LAT = 128
NB = 4
NQ = 4
NO = 1024
HO = NO // 2
HX = LON // 2
SCALE = 1.0 / math.sqrt(M - 1)
UNROLL = 4


def split2(x):
    hi = x.astype(BF16)
    lo = (x - hi.astype(F32)).astype(BF16)
    return hi, lo


def dot6(a, b, dims=((1,), (0,))):
    return lax.dot_general(a, b, (dims, ((), ())), precision=lax.Precision.HIGHEST, preferred_element_type=F32)


def dot3(a, b):
    a0, a1 = split2(a)
    b0, b1 = split2(b)
    return jnp.dot(jnp.concatenate([a0, a0, a1], axis=1), jnp.concatenate([b0, b1, b0], axis=0),
                   preferred_element_type=F32)


def swap_blocks(t, upper, odd):
    u = [None] * 4
    for i in (0, 1):
        u[i] = jnp.where(upper, pltpu.roll(t[i + 2], 64, 1), t[i])
        u[i + 2] = jnp.where(upper, t[i + 2], pltpu.roll(t[i], 64, 1))
    v = [None] * 4
    for i in (0, 2):
        v[i] = jnp.where(odd, pltpu.roll(u[i + 1], 32, 1), u[i])
        v[i + 1] = jnp.where(odd, u[i + 1], pltpu.roll(u[i], 96, 1))
    return v


def kernel(
    ens_hbm, ce_hbm, cn_hbm, pert_hbm, cell_hbm, meas_hbm, var_hbm, count_ref,
    out_ref,
    ens, ce, cn, pert, cell_ref, meas, var, hsrc, hdst, coef, fp, zb, pb, zr, pt, ft, an, rb, mat, rhs, inv,
    load, h_send, h_recv, p_send, p_recv, pf_send, pf_recv, z_send, z_recv, zf_send, zf_recv,
    f_send, f_recv, r_send, r_recv,
):
    g = lax.axis_index("grp")
    s = lax.axis_index("lon")
    my_b, my_q = g // NQ, lax.rem(g, NQ)
    core = lax.rem(g, 2)
    sibling = g + 1 - 2 * core
    east, west = lax.rem(s + 1, NS), lax.rem(s + NS - 1, NS)
    mine = pl.ds(g * MB, MB)

    loads = []
    for i, (src, dst) in enumerate(((ens_hbm, ens), (pert_hbm, pert), (ce_hbm, ce), (cn_hbm, cn),
                                    (cell_hbm, cell_ref), (meas_hbm, meas), (var_hbm, var))):
        loads.append(pltpu.make_async_copy(src, dst, load.at[i]))
        loads[-1].start()

    barrier = pltpu.get_barrier_semaphore()
    for i in range(1, NG):
        pl.semaphore_signal(barrier, inc=1, device_id={"grp": lax.rem(g + i, NG)}, device_id_type=MESH)
    for n in (east, west):
        pl.semaphore_signal(barrier, inc=1, device_id={"lon": n}, device_id_type=MESH)

    def remote(src, dst, send, recv, to):
        return pltpu.make_async_remote_copy(
            src_ref=src, dst_ref=dst, send_sem=send, recv_sem=recv, device_id={"grp": to}, device_id_type=MESH)

    def halo(i, to):
        return pltpu.make_async_remote_copy(
            src_ref=hsrc.at[i], dst_ref=hdst.at[i], send_sem=h_send.at[i], recv_sem=h_recv.at[i],
            device_id={"lon": to}, device_id_type=MESH)

    def pert_copy(to, src):
        half = lax.rem(to, 2)
        return remote(pb.at[to // NQ, half], pt.at[half, pl.ds(src * MB, MB)], p_send.at[to], p_recv.at[src], to)

    def pert_pass(src):
        rows = pt.at[core, pl.ds(src * MB, MB)]
        return remote(rows, rows, pf_send.at[src], pf_recv.at[src], sibling)

    def z_copy(to, src):
        half = lax.rem(to, 2)
        return remote(zb.at[to // NQ, half], zr.at[half, pl.ds(src * MB, MB)], z_send.at[to], z_recv.at[src], to)

    def z_pass(src):
        rows = zr.at[core, pl.ds(src * MB, MB)]
        return remote(rows, rows, zf_send.at[src], zf_recv.at[src], sibling)

    def f_copy(to, src):
        return remote(fp.at[to], ft.at[:, pl.ds(src * MB, MB), :], f_send.at[to], f_recv.at[src], to)

    def r_copy(part, to, src):
        x = pl.ds(part * HX, HX)
        return remote(an.at[x, pl.ds(to * MB, MB), :], rb.at[src, x], r_send.at[part, to], r_recv.at[part, src], to)

    def others(body):
        @pl.loop(1, NG)
        def _(i):
            body(lax.rem(g + i, NG))

    for c in loads:
        c.wait()
    hsrc[0] = ens[:, :, LON - 1, :]
    hsrc[1] = ens[:, :, 0, :]
    for b in range(NB):
        for h in range(2):
            pb[b, h] = pert[:, b, h * HO:(h + 1) * HO]
    pl.semaphore_wait(barrier, NG - 1 + 2)
    halo(0, east).start()
    halo(1, west).start()
    others(lambda to: pert_copy(to, g).start())
    for h in range(2):
        pt[h, mine] = pb[my_b, h]

    lane = lax.broadcasted_iota(jnp.int32, (LON, LAT), 1)
    sub = lax.broadcasted_iota(jnp.int32, (LON, LAT), 0)
    for l in range(LEV):
        c = ce[l]
        coef[0, l] = 1.0 - c * c
        coef[1, l] = 0.5 * (c * c - c)
        coef[2, l] = 0.5 * (c * c + c)
        c = cn[l]
        coef[3, l] = 1.0 - c * c
        coef[4, l] = jnp.where(lane == LAT - 1, 0.0, 0.5 * (c * c - c))
        coef[5, l] = jnp.where(lane == 0, 0.0, 0.5 * (c * c + c))

    halo(0, east).wait()
    halo(1, west).wait()

    upper = lane >= 64
    odd = (lane // 32) % 2 == 1
    for q in range(NQ):
        @pl.loop(0, MB, step=UNROLL)
        def _(m0):
            for i in range(UNROLL):
                m = m0 + i
                tiles = []
                for k in range(4):
                    l = 4 * q + k
                    e = ens[m, l]
                    w_edge = jnp.broadcast_to(hdst[0, m, pl.ds(l, 1), :], (LON, LAT))
                    e_edge = jnp.broadcast_to(hdst[1, m, pl.ds(l, 1), :], (LON, LAT))
                    ww = jnp.where(sub == 0, w_edge, pltpu.roll(e, 1, 0))
                    ee = jnp.where(sub == LON - 1, e_edge, pltpu.roll(e, LON - 1, 0))
                    half = coef[0, l] * e + coef[1, l] * ee + coef[2, l] * ww
                    tiles.append(coef[3, l] * half + coef[4, l] * pltpu.roll(half, LAT - 1, 1)
                                 + coef[5, l] * pltpu.roll(half, 1, 1))
                tiles = swap_blocks(tiles, upper, odd)
                for b in range(NB):
                    for x in range(LON):
                        fp[b * NQ + q, x, pl.ds(m, 1), :] = tiles[b][x:x + 1]

    rows = lax.broadcasted_iota(jnp.int32, (LAT, NO), 0)

    @pl.loop(1, NB + 1)
    def _(i):
        b = lax.rem(my_b + i, NB)
        cell = cell_ref[pl.ds(b, 1), :]
        level = cell // (NS * LON * LAT)
        low = (level % 4) * 32 + cell % 32
        high = (level // 4) * LON + (cell // LAT) % LON
        pick = jnp.where(rows == low, 1.0, 0.0).astype(BF16)
        for o in range(0, NO, 256):
            acc = jnp.zeros((MB, 256), F32)
            hi_o = jnp.broadcast_to(high[:, o:o + 256], (MB, 256))
            pk = pick[:, o:o + 256]
            for q in range(NQ):
                f0, f1 = split2(fp[b * NQ + q].reshape(LON * MB, LAT))
                t = jnp.dot(jnp.concatenate([f0, f1], axis=1), jnp.concatenate([pk, pk], axis=0),
                            preferred_element_type=F32)
                for x in range(LON):
                    acc = acc + jnp.where(hi_o == q * LON + x, t[x * MB:(x + 1) * MB], 0.0)
            zb[b, o // HO, :, o % HO:o % HO + 256] = acc

        @pl.loop(0, NQ)
        def _(j):
            to = b * NQ + lax.rem(my_q + j, NQ)

            @pl.when(to != g)
            def _():
                z_copy(to, g).start()

    for h in range(2):
        zr[h, mine] = zb[my_b, h]
    others(lambda to: f_copy(to, g).start())
    ft[:, mine, :] = fp[g]

    def hand_on(arrived, pass_on):
        pass_on(g).start()

        @pl.loop(1, NG)
        def _(i):
            src = lax.rem(g + NG - i, NG)
            arrived(g, src).wait_recv()

            @pl.when(src != sibling)
            def _():
                pass_on(src).start()

    def handed(pass_on):
        others(lambda src: pass_on(src).wait_recv())

    hand_on(pert_copy, pert_pass)
    hand_on(z_copy, z_pass)

    eye = jnp.where(lax.broadcasted_iota(jnp.int32, (M, M), 0) == lax.broadcasted_iota(jnp.int32, (M, M), 1), 1.0, 0.0)
    slot = lax.broadcasted_iota(jnp.int32, (1, HO), 1)
    count = count_ref[my_b]

    def half_sums(h):
        o = pl.ds(pl.multiple_of(h * HO, HO), HO)
        f = zr[h]
        z = (f - jnp.sum(f, axis=0, keepdims=True) * (1.0 / M)) * SCALE
        w = jnp.where(slot + h * HO < count, 1.0 / var[pl.ds(my_b, 1), o], 0.0)
        d = (meas[pl.ds(my_b, 1), o] + pt[h]) - f
        return dot6(jnp.concatenate([z, d], axis=0), z * w, ((1,), (1,)))

    first = half_sums(core)
    mat[...] = first[:M]
    rhs[...] = first[M:]
    handed(pert_pass)
    handed(z_pass)
    second = half_sums(1 - core)
    spread = mat[...] + second[:M]
    mat[...] = spread + eye
    rhs[...] += second[M:]

    low = 1.0 / (jnp.sqrt(jnp.sum(spread * spread)) * 1.0001 + 1.0)
    k = 4.0 / ((1.0 + low) * (1.0 + low))
    inv[...] = (k * low) * ((1.0 + low) * eye - low * mat[...])

    def newton(dot, low):
        k = 4.0 / ((1.0 + low) * (1.0 + low))
        x = inv[...]
        r = (1.0 + low) * eye - dot(mat[...], x)
        inv[...] = k * dot6(x, r)
        return k * low

    low = lax.fori_loop(0, 5, lambda i, low: newton(dot3, low), k * low)
    low = lax.fori_loop(0, 5, lambda i, low: newton(dot6, low), low)
    x = inv[...] * (2.0 / (1.0 + low))
    y = dot3(rhs[...], x)
    for _ in range(2):
        y = y + dot3(rhs[...] - dot6(y, mat[...]), x)
    y0, y1 = split2(y * SCALE)
    lhs = jnp.concatenate([y0, y0, y1], axis=1)

    others(lambda src: f_copy(g, src).wait_recv())
    for part in range(2):
        for x in range(part * HX, (part + 1) * HX, 2):
            f = jnp.concatenate([ft[x], ft[x + 1]], axis=1)
            a0, a1 = split2(f - jnp.sum(f, axis=0, keepdims=True) * (1.0 / M))
            u = f + jnp.dot(lhs, jnp.concatenate([a0, a1, a0], axis=0), preferred_element_type=F32)
            an[x] = u[:, :LAT]
            an[x + 1] = u[:, LAT:]
        others(lambda to: r_copy(part, to, g).start())
    rb[g] = an[:, mine, :]

    def sent(to):
        pert_copy(to, g).wait_send()
        z_copy(to, g).wait_send()
        f_copy(to, g).wait_send()

        @pl.when(to != sibling)
        def _():
            pert_pass(to).wait_send()
            z_pass(to).wait_send()

    others(sent)
    pert_pass(g).wait_send()
    z_pass(g).wait_send()
    for part in range(2):
        others(lambda src: r_copy(part, g, src).wait_recv())

    back = rb.reshape(NG * LON * MB, LAT)
    for q in range(NQ):
        @pl.loop(0, MB, step=8)
        def _(m0):
            for i in range(8):
                m = m0 + i
                tiles = swap_blocks([back[pl.ds((b * NQ + q) * LON * MB + m, LON, stride=MB), :] for b in range(NB)],
                                    upper, odd)
                for k in range(4):
                    out_ref[m, 4 * q + k] = tiles[k]

    for part in range(2):
        others(lambda to: r_copy(part, to, g).wait_send())


def on_device(ensemble, courant_east, northward_courant, measured, error_variance, sensor_cell, sensor_count, perturbation):
    dma = pltpu.SemaphoreType.DMA
    vm = lambda *shape: pltpu.VMEM(shape, F32)
    hbm = pl.BlockSpec(memory_space=pltpu.HBM)
    return pl.pallas_call(
        kernel,
        out_shape=jax.ShapeDtypeStruct((MB, LEV, LON, LAT), F32),
        in_specs=[hbm] * 7 + [pl.BlockSpec(memory_space=pltpu.SMEM)],
        out_specs=pl.BlockSpec(memory_space=pltpu.VMEM),
        scratch_shapes=[
            vm(MB, LEV, LON, LAT), vm(LEV, LON, LAT), vm(LEV, LON, LAT), vm(MB, NB, NO),
            pltpu.VMEM((NB, NO), jnp.int32), vm(NB, NO), vm(NB, NO),
            vm(2, MB, LEV, LAT), vm(2, MB, LEV, LAT), vm(6, LEV, LON, LAT),
            vm(NG, LON, MB, LAT), vm(NB, 2, MB, HO), vm(NB, 2, MB, HO),
            vm(2, M, HO), vm(2, M, HO), vm(LON, M, LAT), vm(LON, M, LAT), vm(NG, LON, MB, LAT),
            vm(M, M), vm(M, M), vm(M, M),
            dma((7,)), dma((2,)), dma((2,)),
        ] + [dma((NG,))] * 10 + [dma((2, NG))] * 2,
        compiler_params=pltpu.CompilerParams(collective_id=0, has_side_effects=True, vmem_limit_bytes=62 << 20),
    )(ensemble, courant_east, northward_courant, perturbation, sensor_cell, measured, error_variance, sensor_count)


def solution(mesh):
    return jax.shard_map(
        on_device,
        mesh=mesh,
        in_specs=(
            P("grp", None, "lon", None),
            P(None, "lon", None),
            P(None, "lon", None),
            P("lon", None),
            P("lon", None),
            P("lon", None),
            P("lon"),
            P("grp", "lon", None),
        ),
        out_specs=P("grp", None, "lon", None),
        check_vma=False,
    )
```

```python
import functools
import math

import jax
import jax.numpy as jnp
from jax import lax
from jax.experimental import pallas as pl
from jax.experimental.pallas import tpu as pltpu
from jax.sharding import PartitionSpec as P

MESH = pl.DeviceIdType.MESH
F32 = jnp.float32
BF16 = jnp.bfloat16
NG = 16
NS = 16
MB = 16
M = 256
LEV = 16
LON = 8
LAT = 128
NB = 4
NQ = 4
NO = 1024
HO = NO // 2
HX = LON // 2
SCALE = 1.0 / math.sqrt(M - 1)
UNROLL = 4
NR = NG // 2
MR = NR * MB


def split2(x):
    hi = x.astype(BF16)
    lo = (x - hi.astype(F32)).astype(BF16)
    return hi, lo


def device_of(b, q):
    return (q // 2) * NR + b * 2 + q % 2


def dot6(a, b, dims=((1,), (0,))):
    return lax.dot_general(a, b, (dims, ((), ())), precision=lax.Precision.HIGHEST, preferred_element_type=F32)


def dot3(a, b):
    a0, a1 = split2(a)
    b0, b1 = split2(b)
    return jnp.dot(jnp.concatenate([a0, a0, a1], axis=1), jnp.concatenate([b0, b1, b0], axis=0),
                   preferred_element_type=F32)


def swap_blocks(t, upper, odd):
    u = [None] * 4
    for i in (0, 1):
        u[i] = jnp.where(upper, pltpu.roll(t[i + 2], 64, 1), t[i])
        u[i + 2] = jnp.where(upper, t[i + 2], pltpu.roll(t[i], 64, 1))
    v = [None] * 4
    for i in (0, 2):
        v[i] = jnp.where(odd, pltpu.roll(u[i + 1], 32, 1), u[i])
        v[i + 1] = jnp.where(odd, u[i + 1], pltpu.roll(u[i], 96, 1))
    return v


def kernel(
    ens_hbm, ce_hbm, cn_hbm, pert_hbm, cell_hbm, meas_hbm, var_hbm, count_ref,
    out_ref,
    ens, ce, cn, pert, cell_ref, meas, var, hsrc, hdst, coef, fp, zb, pb, zr, pt, ft, an, rb, mat, rhs, inv,
    load, h_send, h_recv, p_send, p_recv, pf_send, pf_recv, z_send, z_recv, zf_send, zf_recv,
    f_send, f_recv, r_send, r_recv, x_send, x_recv,
):
    g = lax.axis_index("grp")
    s = lax.axis_index("lon")
    row, my_b, core = g // NR, lax.rem(g, NR) // 2, lax.rem(g, 2)
    partner = lax.rem(g + NR, NG)
    sibling = g + 1 - 2 * core
    east, west = lax.rem(s + 1, NS), lax.rem(s + NS - 1, NS)
    mine = pl.ds(g * MB, MB)

    loads = []
    for i, (src, dst) in enumerate(((ens_hbm, ens), (pert_hbm, pert), (ce_hbm, ce), (cn_hbm, cn),
                                    (cell_hbm, cell_ref), (meas_hbm, meas), (var_hbm, var))):
        loads.append(pltpu.make_async_copy(src, dst, load.at[i]))
        loads[-1].start()

    barrier = pltpu.get_barrier_semaphore()
    for i in range(1, NG):
        pl.semaphore_signal(barrier, inc=1, device_id={"grp": lax.rem(g + i, NG)}, device_id_type=MESH)
    for n in (east, west):
        pl.semaphore_signal(barrier, inc=1, device_id={"lon": n}, device_id_type=MESH)

    def remote(src, dst, send, recv, to):
        return pltpu.make_async_remote_copy(
            src_ref=src, dst_ref=dst, send_sem=send, recv_sem=recv, device_id={"grp": to}, device_id_type=MESH)

    def halo(i, c, to):
        rows = pl.ds(c * UNROLL, UNROLL)
        return pltpu.make_async_remote_copy(
            src_ref=hsrc.at[i, rows], dst_ref=hdst.at[i, rows], send_sem=h_send.at[i, c], recv_sem=h_recv.at[i, c],
            device_id={"lon": to}, device_id_type=MESH)

    def pert_copy(to, src):
        half = lax.rem(to, 2)
        return remote(pb.at[lax.rem(to, NR) // 2, half], pt.at[half, pl.ds(lax.rem(src, NR) * MB, MB)],
                      p_send.at[to], p_recv.at[src], to)

    def pert_pass(src):
        rows = pt.at[core, pl.ds(lax.rem(src, NR) * MB, MB)]
        return remote(rows, rows, pf_send.at[src], pf_recv.at[src], sibling)

    def z_copy(to, src):
        half = lax.rem(to, 2)
        return remote(zb.at[lax.rem(to, NR) // 2, half], zr.at[half, pl.ds(src * MB, MB)], z_send.at[to], z_recv.at[src], to)

    def z_pass(src):
        rows = zr.at[core, pl.ds(src * MB, MB)]
        return remote(rows, rows, zf_send.at[src], zf_recv.at[src], sibling)

    def f_copy(to, src):
        return remote(fp.at[to], ft.at[:, pl.ds(src * MB, MB), :], f_send.at[to], f_recv.at[src], to)

    def r_copy(part, to, src):
        x = pl.ds(part * HX, HX)
        return remote(an.at[x, pl.ds(to * MB, MB), :], rb.at[src, x], r_send.at[part, to], r_recv.at[part, src], to)

    def rhs_copy(to_row):
        rows = rhs.at[pl.ds((1 - to_row) * MR + core * (MR // 2), MR // 2)]
        return remote(rows, rows, x_send.at[0], x_recv.at[0], partner)

    def rhs_pass(half):
        rows = rhs.at[pl.ds((1 - row) * MR + half * (MR // 2), MR // 2)]
        return remote(rows, rows, x_send.at[1], x_recv.at[1], sibling)

    def stepped(i, dy, sign):
        k = i // 4
        dx = lax.rem(1 + 2 * k + k // 2, 4)
        x = lax.rem(my_b + 4 + sign * dx, 4)
        dc = 1 - lax.rem(i, 4) // 2
        return lax.rem(row + dy, 2) * NR + x * 2 + lax.rem(core + dc, 2)

    def same_row(body, sign=1):
        @pl.loop(0, NR - 1)
        def _(i):
            body(stepped(2 * i, 0, sign))

    def others(body, sign=1, first=0, last=NG - 1):
        @pl.loop(first, last)
        def _(i):
            body(stepped(i, 1 - lax.rem(i, 2), sign))

    for c in loads:
        c.wait()
    hsrc[0] = ens[:, :, LON - 1, :]
    hsrc[1] = ens[:, :, 0, :]
    for b in range(NB):
        for h in range(2):
            pb[b, h] = pert[:, b, h * HO:(h + 1) * HO]
    pl.semaphore_wait(barrier, NG - 1 + 2)

    @pl.loop(0, MB // UNROLL)
    def _(c):
        halo(0, c, east).start()
        halo(1, c, west).start()

    same_row(lambda to: pert_copy(to, g).start())
    for h in range(2):
        pt[h, pl.ds(lax.rem(g, NR) * MB, MB)] = pb[my_b, h]

    lane = lax.broadcasted_iota(jnp.int32, (LON, LAT), 1)
    sub = lax.broadcasted_iota(jnp.int32, (LON, LAT), 0)
    for l in range(LEV):
        c = ce[l]
        coef[0, l] = 1.0 - c * c
        coef[1, l] = 0.5 * (c * c - c)
        coef[2, l] = 0.5 * (c * c + c)
        c = cn[l]
        coef[3, l] = 1.0 - c * c
        coef[4, l] = jnp.where(lane == LAT - 1, 0.0, 0.5 * (c * c - c))
        coef[5, l] = jnp.where(lane == 0, 0.0, 0.5 * (c * c + c))


    upper = lane >= 64
    odd = (lane // 32) % 2 == 1

    @pl.loop(0, MB // UNROLL)
    def _(c):
        halo(0, c, east).wait()
        halo(1, c, west).wait()
        for q in range(NQ):
            for i in range(UNROLL):
                m = c * UNROLL + i
                tiles = []
                for k in range(4):
                    l = 4 * q + k
                    e = ens[m, l]
                    w_edge = jnp.broadcast_to(hdst[0, m, pl.ds(l, 1), :], (LON, LAT))
                    e_edge = jnp.broadcast_to(hdst[1, m, pl.ds(l, 1), :], (LON, LAT))
                    ww = jnp.where(sub == 0, w_edge, pltpu.roll(e, 1, 0))
                    ee = jnp.where(sub == LON - 1, e_edge, pltpu.roll(e, LON - 1, 0))
                    half = coef[0, l] * e + coef[1, l] * ee + coef[2, l] * ww
                    tiles.append(coef[3, l] * half + coef[4, l] * pltpu.roll(half, LAT - 1, 1)
                                 + coef[5, l] * pltpu.roll(half, 1, 1))
                tiles = swap_blocks(tiles, upper, odd)
                for b in range(NB):
                    for x in range(LON):
                        fp[device_of(b, q), x, pl.ds(m, 1), :] = tiles[b][x:x + 1]

    rows = lax.broadcasted_iota(jnp.int32, (LAT, NO), 0)

    @pl.loop(0, NB)
    def _(k):
        b = lax.rem(my_b + lax.rem(1 + 2 * k + k // 2, 4), NB)
        cell = cell_ref[pl.ds(b, 1), :]
        level = cell // (NS * LON * LAT)
        low = (level % 4) * 32 + cell % 32
        high = (level // 4) * LON + (cell // LAT) % LON
        pick = jnp.where(rows == low, 1.0, 0.0).astype(BF16)
        for o in range(0, NO, 256):
            acc = jnp.zeros((MB, 256), F32)
            hi_o = jnp.broadcast_to(high[:, o:o + 256], (MB, 256))
            pk = pick[:, o:o + 256]
            for q in range(NQ):
                f0, f1 = split2(fp[device_of(b, q)].reshape(LON * MB, LAT))
                t = jnp.dot(jnp.concatenate([f0, f1], axis=1), jnp.concatenate([pk, pk], axis=0),
                            preferred_element_type=F32)
                for x in range(LON):
                    acc = acc + jnp.where(hi_o == q * LON + x, t[x * MB:(x + 1) * MB], 0.0)
            zb[b, o // HO, :, o % HO:o % HO + 256] = acc

        @pl.loop(0, NQ)
        def _(j):
            to = stepped(4 * k + j, 1 - lax.rem(j, 2), 1)

            @pl.when(to != g)
            def _():
                z_copy(to, g).start()

    for h in range(2):
        zr[h, mine] = zb[my_b, h]

    def hand_on(sources, arrived, pass_on):
        pass_on(g).start()

        def arrive(src):
            arrived(g, src).wait_recv()

            @pl.when(src != sibling)
            def _():
                pass_on(src).start()

        sources(arrive, -1)

    hand_on(same_row, pert_copy, pert_pass)
    hand_on(others, z_copy, z_pass)
    others(lambda to: f_copy(to, g).start(), last=8)
    ft[:, mine, :] = fp[g]

    eye = jnp.where(lax.broadcasted_iota(jnp.int32, (M, M), 0) == lax.broadcasted_iota(jnp.int32, (M, M), 1), 1.0, 0.0)
    slot = lax.broadcasted_iota(jnp.int32, (1, HO), 1)
    count = count_ref[my_b]
    row_rows = pl.ds(row * MR, MR)

    def half_sums(h):
        o = pl.ds(pl.multiple_of(h * HO, HO), HO)
        f = zr[h]
        z = (f - jnp.sum(f, axis=0, keepdims=True) * (1.0 / M)) * SCALE
        w = jnp.where(slot + h * HO < count, 1.0 / var[pl.ds(my_b, 1), o], 0.0)
        d = (meas[pl.ds(my_b, 1), o] + pt[h]) - zr[h, row_rows]
        return dot6(jnp.concatenate([z, d], axis=0), z * w, ((1,), (1,)))

    first = half_sums(core)
    mat[...] = first[:M]
    rhs[row_rows] = first[M:]
    same_row(lambda src: pert_pass(src).wait_recv())
    others(lambda src: z_pass(src).wait_recv())
    second = half_sums(1 - core)
    spread = mat[...] + second[:M]
    mat[...] = spread + eye
    rhs[row_rows] += second[M:]
    rhs_copy(1 - row).start()
    others(lambda to: f_copy(to, g).start(), first=8)

    low = 1.0 / (jnp.sqrt(jnp.sum(spread * spread)) * 1.0001 + 1.0)
    k = 4.0 / ((1.0 + low) * (1.0 + low))
    inv[...] = (k * low) * ((1.0 + low) * eye - low * mat[...])

    def newton(dot, low):
        k = 4.0 / ((1.0 + low) * (1.0 + low))
        x = inv[...]
        r = (1.0 + low) * eye - dot(mat[...], x)
        inv[...] = k * dot6(x, r)
        return k * low

    low = lax.fori_loop(0, 5, lambda i, low: newton(dot3, low), k * low)
    low = lax.fori_loop(0, 4, lambda i, low: newton(dot6, low), low)
    rhs_copy(row).wait_recv()
    rhs_pass(core).start()
    low = newton(dot6, low)
    x = inv[...] * (2.0 / (1.0 + low))
    rhs_pass(1 - core).wait_recv()
    y = dot3(rhs[...], x)
    for _ in range(2):
        y = y + dot3(rhs[...] - dot6(y, mat[...]), x)
    y0, y1 = split2(y * SCALE)
    lhs = jnp.concatenate([y0, y0, y1], axis=1)

    others(lambda src: f_copy(g, src).wait_recv())
    for part in range(2):
        for x in range(part * HX, (part + 1) * HX, 2):
            f = jnp.concatenate([ft[x], ft[x + 1]], axis=1)
            a0, a1 = split2(f - jnp.sum(f, axis=0, keepdims=True) * (1.0 / M))
            u = f + jnp.dot(lhs, jnp.concatenate([a0, a1, a0], axis=0), preferred_element_type=F32)
            an[x] = u[:, :LAT]
            an[x + 1] = u[:, LAT:]
        others(lambda to: r_copy(part, to, g).start())
    rb[g] = an[:, mine, :]

    def sent(to):
        z_copy(to, g).wait_send()
        f_copy(to, g).wait_send()

        @pl.when(to != sibling)
        def _():
            z_pass(to).wait_send()

    def pert_sent(to):
        pert_copy(to, g).wait_send()

        @pl.when(to != sibling)
        def _():
            pert_pass(to).wait_send()

    others(sent)
    same_row(pert_sent)
    rhs_copy(1 - row).wait_send()
    rhs_pass(core).wait_send()
    pert_pass(g).wait_send()
    z_pass(g).wait_send()
    for part in range(2):
        others(lambda src: r_copy(part, g, src).wait_recv())

    back = rb.reshape(NG * LON * MB, LAT)
    for q in range(NQ):
        @pl.loop(0, MB, step=8)
        def _(m0):
            for i in range(8):
                m = m0 + i
                tiles = swap_blocks([back[pl.ds(device_of(b, q) * LON * MB + m, LON, stride=MB), :] for b in range(NB)],
                                    upper, odd)
                for k in range(4):
                    out_ref[m, 4 * q + k] = tiles[k]

    for part in range(2):
        others(lambda to: r_copy(part, to, g).wait_send())


def on_device(ensemble, courant_east, northward_courant, measured, error_variance, sensor_cell, sensor_count, perturbation):
    dma = pltpu.SemaphoreType.DMA
    vm = lambda *shape: pltpu.VMEM(shape, F32)
    hbm = pl.BlockSpec(memory_space=pltpu.HBM)
    return pl.pallas_call(
        kernel,
        out_shape=jax.ShapeDtypeStruct((MB, LEV, LON, LAT), F32),
        in_specs=[hbm] * 7 + [pl.BlockSpec(memory_space=pltpu.SMEM)],
        out_specs=pl.BlockSpec(memory_space=pltpu.VMEM),
        scratch_shapes=[
            vm(MB, LEV, LON, LAT), vm(LEV, LON, LAT), vm(LEV, LON, LAT), vm(MB, NB, NO),
            pltpu.VMEM((NB, NO), jnp.int32), vm(NB, NO), vm(NB, NO),
            vm(2, MB, LEV, LAT), vm(2, MB, LEV, LAT), vm(6, LEV, LON, LAT),
            vm(NG, LON, MB, LAT), vm(NB, 2, MB, HO), vm(NB, 2, MB, HO),
            vm(2, M, HO), vm(2, MR, HO), vm(LON, M, LAT), vm(LON, M, LAT), vm(NG, LON, MB, LAT),
            vm(M, M), vm(M, M), vm(M, M),
            dma((7,)), dma((2, MB // UNROLL)), dma((2, MB // UNROLL)),
        ] + [dma((NG,))] * 10 + [dma((2, NG))] * 2 + [dma((2,))] * 2,
        compiler_params=pltpu.CompilerParams(collective_id=0, has_side_effects=True, vmem_limit_bytes=62 << 20),
    )(ensemble, courant_east, northward_courant, perturbation, sensor_cell, measured, error_variance, sensor_count)


def solution(mesh):
    return jax.shard_map(
        on_device,
        mesh=mesh,
        in_specs=(
            P("grp", None, "lon", None),
            P(None, "lon", None),
            P(None, "lon", None),
            P("lon", None),
            P("lon", None),
            P("lon", None),
            P("lon"),
            P("grp", "lon", None),
        ),
        out_specs=P("grp", None, "lon", None),
        check_vma=False,
    )
```

```python
import functools
import math

import jax
import jax.numpy as jnp
from jax import lax
from jax.experimental import pallas as pl
from jax.experimental.pallas import tpu as pltpu
from jax.sharding import PartitionSpec as P

MESH = pl.DeviceIdType.MESH
F32 = jnp.float32
BF16 = jnp.bfloat16
NG = 16
NS = 16
MB = 16
M = 256
LEV = 16
LON = 8
LAT = 128
NB = 4
NQ = 4
NO = 1024
HO = NO // 2
HX = LON // 2
SCALE = 1.0 / math.sqrt(M - 1)
UNROLL = 4
NR = NG // 2
MR = NR * MB


def split2(x):
    hi = x.astype(BF16)
    lo = (x - hi.astype(F32)).astype(BF16)
    return hi, lo


def device_of(b, q):
    return (q // 2) * NR + b * 2 + q % 2


def dot6(a, b, dims=((1,), (0,))):
    return lax.dot_general(a, b, (dims, ((), ())), precision=lax.Precision.HIGHEST, preferred_element_type=F32)


def split3(x):
    x0 = x.astype(BF16)
    rest = x - x0.astype(F32)
    x1, x2 = split2(rest)
    return x0, x1, x2


def left3(p):
    return jnp.concatenate([p[0], p[0], p[1]], axis=1)


def right3(p):
    return jnp.concatenate([p[0], p[1], p[0]], axis=0)


def left6(p):
    return jnp.concatenate([p[0], p[0], p[0], p[1], p[1], p[2]], axis=1)


def right6(p):
    return jnp.concatenate([p[0], p[1], p[2], p[0], p[1], p[0]], axis=0)


def mul(a, b):
    return jnp.dot(a, b, preferred_element_type=F32)


def dot3(a, b):
    a0, a1 = split2(a)
    b0, b1 = split2(b)
    return jnp.dot(jnp.concatenate([a0, a0, a1], axis=1), jnp.concatenate([b0, b1, b0], axis=0),
                   preferred_element_type=F32)


def swap_blocks(t, upper, odd):
    u = [None] * 4
    for i in (0, 1):
        u[i] = jnp.where(upper, pltpu.roll(t[i + 2], 64, 1), t[i])
        u[i + 2] = jnp.where(upper, t[i + 2], pltpu.roll(t[i], 64, 1))
    v = [None] * 4
    for i in (0, 2):
        v[i] = jnp.where(odd, pltpu.roll(u[i + 1], 32, 1), u[i])
        v[i + 1] = jnp.where(odd, u[i + 1], pltpu.roll(u[i], 96, 1))
    return v


def kernel(
    ens_hbm, ce_hbm, cn_hbm, pert_hbm, cell_hbm, meas_hbm, var_hbm, count_ref,
    rb,
    ens, ce, cn, pert, cell_ref, meas, var, hsrc, hdst, coef, fp, zb, pb, zr, pt, ft, an, mat, rhs, inv, mp, own_sums, other_sums,
    load, h_send, h_recv, p_send, p_recv, z_send, z_recv,
    f_send, f_recv, r_send, r_recv, x_send, x_recv, s_send, s_recv,
):
    g = lax.axis_index("grp")
    s = lax.axis_index("lon")
    row, my_b, core = g // NR, lax.rem(g, NR) // 2, lax.rem(g, 2)
    partner = lax.rem(g + NR, NG)
    sibling = g + 1 - 2 * core
    east, west = lax.rem(s + 1, NS), lax.rem(s + NS - 1, NS)
    mine = pl.ds(g * MB, MB)

    barrier = pltpu.get_barrier_semaphore()
    for i in range(1, NG):
        pl.semaphore_signal(barrier, inc=1, device_id={"grp": lax.rem(g + i, NG)}, device_id_type=MESH)
    for n in (east, west):
        pl.semaphore_signal(barrier, inc=1, device_id={"lon": n}, device_id_type=MESH)

    loads = []
    for i, (src, dst) in enumerate(((ens_hbm, ens), (pert_hbm, pert), (ce_hbm, ce), (cn_hbm, cn),
                                    (cell_hbm, cell_ref), (meas_hbm, meas), (var_hbm, var))):
        loads.append(pltpu.make_async_copy(src, dst, load.at[i]))
        loads[-1].start()

    def remote(src, dst, send, recv, to):
        return pltpu.make_async_remote_copy(
            src_ref=src, dst_ref=dst, send_sem=send, recv_sem=recv, device_id={"grp": to}, device_id_type=MESH)

    def halo(i, c, to):
        rows = pl.ds(c * UNROLL, UNROLL)
        return pltpu.make_async_remote_copy(
            src_ref=hsrc.at[i, rows], dst_ref=hdst.at[i, rows], send_sem=h_send.at[i, c], recv_sem=h_recv.at[i, c],
            device_id={"lon": to}, device_id_type=MESH)

    def pert_copy(to, src):
        half = lax.rem(to, 2)
        return remote(pb.at[lax.rem(to, NR) // 2, half], pt.at[pl.ds(lax.rem(src, NR) * MB, MB)],
                      p_send.at[to], p_recv.at[src], to)

    def z_copy(to, src):
        half = lax.rem(to, 2)
        return remote(zb.at[lax.rem(to, NR) // 2, half], zr.at[pl.ds(src * MB, MB)], z_send.at[to], z_recv.at[src], to)

    def sums_copy(i):
        rows = pl.ds(i * M, M if i == 0 else MR)
        return remote(own_sums.at[rows], other_sums.at[rows], s_send.at[i], s_recv.at[i], sibling)

    def f_copy(to, src):
        return remote(fp.at[to], ft.at[:, pl.ds(src * MB, MB), :], f_send.at[to], f_recv.at[src], to)

    def r_copy(part, to, src):
        x = pl.ds(part * HX, HX)
        return remote(an.at[x, pl.ds(to * MB, MB), :], rb.at[src, x], r_send.at[part, to], r_recv.at[part, src], to)

    def rhs_copy(to_row):
        rows = rhs.at[pl.ds((1 - to_row) * MR + core * (MR // 2), MR // 2)]
        return remote(rows, rows, x_send.at[0], x_recv.at[0], partner)

    def rhs_pass(half):
        rows = rhs.at[pl.ds((1 - row) * MR + half * (MR // 2), MR // 2)]
        return remote(rows, rows, x_send.at[1], x_recv.at[1], sibling)

    def stepped(i, dy, sign):
        k = i // 4
        dx = (1 + 2 * k + k // 2) % 4
        x = lax.rem(my_b + 4 + sign * dx, 4)
        dc = 1 - i % 4 // 2
        return lax.rem(row + dy, 2) * NR + x * 2 + lax.rem(core + dc, 2)

    order = {sign: [stepped(i, 1 - i % 2, sign) for i in range(NG)] for sign in (1, -1)}

    def same_row(body, sign=1):
        for i in range(NR - 1):
            body(order[sign][2 * i + 1])

    def others(body, sign=1, first=0, last=NG - 1):
        for i in range(first, last):
            body(order[sign][i])

    loads[0].wait()
    hsrc[0] = ens[:, :, LON - 1, :]
    hsrc[1] = ens[:, :, 0, :]
    pl.semaphore_wait(barrier, NG - 1 + 2)

    @pl.loop(0, MB // UNROLL)
    def _(c):
        halo(0, c, east).start()
        halo(1, c, west).start()

    for c in loads[1:]:
        c.wait()
    for b in range(NB):
        for h in range(2):
            pb[b, h] = pert[:, b, h * HO:(h + 1) * HO]
    same_row(lambda to: pert_copy(to, g).start())
    pt[pl.ds(lax.rem(g, NR) * MB, MB)] = pb[my_b, core]

    lane = lax.broadcasted_iota(jnp.int32, (LON, LAT), 1)
    sub = lax.broadcasted_iota(jnp.int32, (LON, LAT), 0)
    for l in range(LEV):
        c = ce[l]
        coef[0, l] = 1.0 - c * c
        coef[1, l] = 0.5 * (c * c - c)
        coef[2, l] = 0.5 * (c * c + c)
        c = cn[l]
        coef[3, l] = 1.0 - c * c
        coef[4, l] = jnp.where(lane == LAT - 1, 0.0, 0.5 * (c * c - c))
        coef[5, l] = jnp.where(lane == 0, 0.0, 0.5 * (c * c + c))


    upper = lane >= 64
    odd = (lane // 32) % 2 == 1

    @pl.loop(0, MB // UNROLL)
    def _(c):
        halo(0, c, east).wait()
        halo(1, c, west).wait()
        for q in range(NQ):
            for i in range(UNROLL):
                m = c * UNROLL + i
                tiles = []
                for k in range(4):
                    l = 4 * q + k
                    e = ens[m, l]
                    w_edge = jnp.broadcast_to(hdst[0, m, pl.ds(l, 1), :], (LON, LAT))
                    e_edge = jnp.broadcast_to(hdst[1, m, pl.ds(l, 1), :], (LON, LAT))
                    ww = jnp.where(sub == 0, w_edge, pltpu.roll(e, 1, 0))
                    ee = jnp.where(sub == LON - 1, e_edge, pltpu.roll(e, LON - 1, 0))
                    half = coef[0, l] * e + coef[1, l] * ee + coef[2, l] * ww
                    tiles.append(coef[3, l] * half + coef[4, l] * pltpu.roll(half, LAT - 1, 1)
                                 + coef[5, l] * pltpu.roll(half, 1, 1))
                tiles = swap_blocks(tiles, upper, odd)
                for b in range(NB):
                    for x in range(LON):
                        fp[device_of(b, q), x, pl.ds(m, 1), :] = tiles[b][x:x + 1]

    rows = lax.broadcasted_iota(jnp.int32, (LAT, NO), 0)

    for k in range(NB):
        b = lax.rem(my_b + (1 + 2 * k + k // 2) % 4, NB)
        cell = cell_ref[pl.ds(b, 1), :]
        level = cell // (NS * LON * LAT)
        low = (level % 4) * 32 + cell % 32
        high = (level // 4) * LON + (cell // LAT) % LON
        pick = jnp.where(rows == low, 1.0, 0.0).astype(BF16)
        for o in range(0, NO, 256):
            acc = jnp.zeros((MB, 256), F32)
            hi_o = jnp.broadcast_to(high[:, o:o + 256], (MB, 256))
            pk = pick[:, o:o + 256]
            for q in range(NQ):
                f0, f1 = split2(fp[device_of(b, q)].reshape(LON * MB, LAT))
                t = jnp.dot(jnp.concatenate([f0, f1], axis=1), jnp.concatenate([pk, pk], axis=0),
                            preferred_element_type=F32)
                for x in range(LON):
                    acc = acc + jnp.where(hi_o == q * LON + x, t[x * MB:(x + 1) * MB], 0.0)
            zb[b, o // HO, :, o % HO:o % HO + 256] = acc

        for j in range(NQ):
            if 4 * k + j < NG - 1:
                z_copy(order[1][4 * k + j], g).start()

    zr[mine] = zb[my_b, core]

    same_row(lambda src: pert_copy(g, src).wait_recv(), -1)
    others(lambda src: z_copy(g, src).wait_recv(), -1)
    others(lambda to: f_copy(to, g).start(), last=8)
    ft[:, mine, :] = fp[g]

    eye = jnp.where(lax.broadcasted_iota(jnp.int32, (M, M), 0) == lax.broadcasted_iota(jnp.int32, (M, M), 1), 1.0, 0.0)
    slot = lax.broadcasted_iota(jnp.int32, (1, HO), 1)
    count = count_ref[my_b]
    row_rows = pl.ds(row * MR, MR)

    o = pl.ds(pl.multiple_of(core * HO, HO), HO)
    f = zr[...]
    z = (f - jnp.sum(f, axis=0, keepdims=True) * (1.0 / M)) * SCALE
    zw = z * jnp.where(slot + core * HO < count, 1.0 / var[pl.ds(my_b, 1), o], 0.0)
    own_sums[:M] = dot6(z, zw, ((1,), (1,)))
    sums_copy(0).start()
    d = (meas[pl.ds(my_b, 1), o] + pt[...]) - zr[row_rows]
    own_sums[M:] = dot6(d, zw, ((1,), (1,)))
    sums_copy(1).start()
    sums_copy(0).wait_recv()
    spread = own_sums[:M] + other_sums[:M]
    mat[...] = spread + eye

    low = 1.0 / (jnp.sqrt(jnp.sum(spread * spread)) * 1.0001 + 1.0)
    k = 4.0 / ((1.0 + low) * (1.0 + low))
    inv[...] = (k * low) * ((1.0 + low) * eye - low * mat[...])

    pieces = split3(mat[...])
    for i in range(3):
        mp[:, i * M:(i + 1) * M] = pieces[i]

    def newton(exact, low):
        k = 4.0 / ((1.0 + low) * (1.0 + low))
        m = [mp[:, i * M:(i + 1) * M] for i in range(3)]
        x = split3(inv[...])
        r = (1.0 + low) * eye - (mul(left6(x), right6(m)) if exact else mul(left3(x), right3(m)))
        inv[...] = k * mul(left6(split3(r)), right6(x))
        return k * low

    sums_copy(1).wait_recv()
    rhs[row_rows] = own_sums[M:] + other_sums[M:]
    rhs_copy(1 - row).start()
    others(lambda to: f_copy(to, g).start(), first=8)
    low = lax.fori_loop(0, 7, lambda i, low: newton(False, low), k * low)
    low = lax.fori_loop(0, 3, lambda i, low: newton(True, low), low)
    rhs_copy(row).wait_recv()
    rhs_pass(core).start()
    x = right3(split2(inv[...] * (2.0 / (1.0 + low))))
    rhs_pass(1 - core).wait_recv()
    m = right6([mp[:, i * M:(i + 1) * M] for i in range(3)])
    y = mul(left3(split2(rhs[...])), x)
    for _ in range(2):
        y = y + mul(left3(split2(rhs[...] - mul(left6(split3(y)), m))), x)
    y0, y1 = split2(y * SCALE)
    lhs = jnp.concatenate([y0, y0, y1], axis=1)

    others(lambda src: f_copy(g, src).wait_recv())
    for part in range(2):
        for x in range(part * HX, (part + 1) * HX, 2):
            f = jnp.concatenate([ft[x], ft[x + 1]], axis=1)
            a0, a1 = split2(f - jnp.sum(f, axis=0, keepdims=True) * (1.0 / M))
            u = f + jnp.dot(lhs, jnp.concatenate([a0, a1, a0], axis=0), preferred_element_type=F32)
            an[x] = u[:, :LAT]
            an[x + 1] = u[:, LAT:]
        others(lambda to: r_copy(part, to, g).start())
    own = pltpu.make_async_copy(an.at[:, mine, :], rb.at[g], load.at[0])
    own.start()

    def sent(to):
        z_copy(to, g).wait_send()
        f_copy(to, g).wait_send()

    others(sent)
    same_row(lambda to: pert_copy(to, g).wait_send())
    for i in range(2):
        sums_copy(i).wait_send()
    rhs_copy(1 - row).wait_send()
    rhs_pass(core).wait_send()
    for part in range(2):
        others(lambda src: r_copy(part, g, src).wait_recv())

    for part in range(2):
        others(lambda to: r_copy(part, to, g).wait_send())
    own.wait()


def unpack_kernel(rb, out_hbm, buf, out, loaded, stored):
    lane = lax.broadcasted_iota(jnp.int32, (LON, LAT), 1)
    upper = lane >= 64
    odd = (lane // 32) % 2 == 1

    def load(q):
        return pltpu.make_async_copy(rb.at[q // 2, :, q % 2], buf.at[q], loaded.at[q])

    def store(q):
        levels = pl.ds(q * (LEV // NQ), LEV // NQ)
        return pltpu.make_async_copy(out.at[:, levels], out_hbm.at[:, levels], stored.at[q])

    for q in range(NQ):
        load(q).start()
    back = buf.reshape(NQ * NB * LON * MB, LAT)
    for q in range(NQ):
        load(q).wait()

        @pl.loop(0, MB, step=8)
        def _(m0):
            for i in range(8):
                m = m0 + i
                tiles = swap_blocks([back[pl.ds((q * NB + b) * LON * MB + m, LON, stride=MB), :] for b in range(NB)],
                                    upper, odd)
                for k in range(4):
                    out[m, 4 * q + k] = tiles[k]

        store(q).start()
    for q in range(NQ):
        store(q).wait()


def on_device(ensemble, courant_east, northward_courant, measured, error_variance, sensor_cell, sensor_count, perturbation):
    dma = pltpu.SemaphoreType.DMA
    vm = lambda *shape: pltpu.VMEM(shape, F32)
    hbm = pl.BlockSpec(memory_space=pltpu.HBM)
    back = pl.pallas_call(
        kernel,
        out_shape=jax.ShapeDtypeStruct((NG, LON, MB, LAT), F32),
        in_specs=[hbm] * 7 + [pl.BlockSpec(memory_space=pltpu.SMEM)],
        out_specs=hbm,
        scratch_shapes=[
            vm(MB, LEV, LON, LAT), vm(LEV, LON, LAT), vm(LEV, LON, LAT), vm(MB, NB, NO),
            pltpu.VMEM((NB, NO), jnp.int32), vm(NB, NO), vm(NB, NO),
            vm(2, MB, LEV, LAT), vm(2, MB, LEV, LAT), vm(6, LEV, LON, LAT),
            vm(NG, LON, MB, LAT), vm(NB, 2, MB, HO), vm(NB, 2, MB, HO),
            vm(M, HO), vm(MR, HO), vm(LON, M, LAT), vm(LON, M, LAT),
            vm(M, M), vm(M, M), vm(M, M), pltpu.VMEM((M, 3 * M), BF16), vm(M + MR, M), vm(M + MR, M),
            dma((7,)), dma((2, MB // UNROLL)), dma((2, MB // UNROLL)),
        ] + [dma((NG,))] * 6 + [dma((2, NG))] * 2 + [dma((2,))] * 4,
        compiler_params=pltpu.CompilerParams(collective_id=0, has_side_effects=True, vmem_limit_bytes=62 << 20),
    )(ensemble, courant_east, northward_courant, perturbation, sensor_cell, measured, error_variance, sensor_count)
    return pl.pallas_call(
        unpack_kernel,
        out_shape=jax.ShapeDtypeStruct((MB, LEV, LON, LAT), F32),
        in_specs=[hbm],
        out_specs=hbm,
        scratch_shapes=[vm(NQ, NB, LON, MB, LAT), vm(MB, LEV, LON, LAT), dma((NQ,)), dma((NQ,))],
        compiler_params=pltpu.CompilerParams(vmem_limit_bytes=62 << 20),
    )(back.reshape(2, NB, 2, LON, MB, LAT))


def solution(mesh):
    return jax.shard_map(
        on_device,
        mesh=mesh,
        in_specs=(
            P("grp", None, "lon", None),
            P(None, "lon", None),
            P(None, "lon", None),
            P("lon", None),
            P("lon", None),
            P("lon", None),
            P("lon"),
            P("grp", "lon", None),
        ),
        out_specs=P("grp", None, "lon", None),
        check_vma=False,
    )
```

```python
import functools
import math

import jax
import jax.numpy as jnp
from jax import lax
from jax.experimental import pallas as pl
from jax.experimental.pallas import tpu as pltpu
from jax.sharding import PartitionSpec as P

MESH = pl.DeviceIdType.MESH
F32 = jnp.float32
BF16 = jnp.bfloat16
NG = 16
NS = 16
MB = 16
M = 256
LEV = 16
LON = 8
LAT = 128
NB = 4
NQ = 4
NO = 1024
HO = NO // 2
HX = LON // 2
SCALE = 1.0 / math.sqrt(M - 1)
UNROLL = 2
NR = NG // 2
MR = NR * MB


def split2(x):
    hi = x.astype(BF16)
    lo = (x - hi.astype(F32)).astype(BF16)
    return hi, lo


def device_of(b, q):
    return (q // 2) * NR + b * 2 + q % 2


def dot6(a, b, dims=((1,), (0,))):
    return lax.dot_general(a, b, (dims, ((), ())), precision=lax.Precision.HIGHEST, preferred_element_type=F32)


def split3(x):
    x0 = x.astype(BF16)
    rest = x - x0.astype(F32)
    x1, x2 = split2(rest)
    return x0, x1, x2


def left3(p):
    return jnp.concatenate([p[0], p[0], p[1]], axis=1)


def right3(p):
    return jnp.concatenate([p[0], p[1], p[0]], axis=0)


def left5(p):
    return jnp.concatenate([p[0], p[0], p[0], p[1], p[1]], axis=1)


def right5(p):
    return jnp.concatenate([p[0], p[1], p[2], p[0], p[1]], axis=0)


def left6(p):
    return jnp.concatenate([p[0], p[0], p[0], p[1], p[1], p[2]], axis=1)


def right6(p):
    return jnp.concatenate([p[0], p[1], p[2], p[0], p[1], p[0]], axis=0)


def mul(a, b):
    return jnp.dot(a, b, preferred_element_type=F32)


def dot3(a, b):
    a0, a1 = split2(a)
    b0, b1 = split2(b)
    return jnp.dot(jnp.concatenate([a0, a0, a1], axis=1), jnp.concatenate([b0, b1, b0], axis=0),
                   preferred_element_type=F32)


def swap_blocks(t, upper, odd):
    u = [None] * 4
    for i in (0, 1):
        u[i] = jnp.where(upper, pltpu.roll(t[i + 2], 64, 1), t[i])
        u[i + 2] = jnp.where(upper, t[i + 2], pltpu.roll(t[i], 64, 1))
    v = [None] * 4
    for i in (0, 2):
        v[i] = jnp.where(odd, pltpu.roll(u[i + 1], 32, 1), u[i])
        v[i + 1] = jnp.where(odd, u[i + 1], pltpu.roll(u[i], 96, 1))
    return v


def kernel(
    ens_hbm, ce_hbm, cn_hbm, pert_hbm, cell_hbm, meas_hbm, var_hbm, count_ref,
    rb,
    ens, ce, cn, pert, cell_ref, meas, var, hsrc, hdst, coef, fp, zb, pb, zr, pt, ft, an, mat, rhs, inv, mp, own_sums, other_sums,
    load, h_send, h_recv, p_send, p_recv, z_send, z_recv,
    f_send, f_recv, r_send, r_recv, x_send, x_recv, s_send, s_recv,
):
    g = lax.axis_index("grp")
    s = lax.axis_index("lon")
    row, my_b, core = g // NR, lax.rem(g, NR) // 2, lax.rem(g, 2)
    partner = lax.rem(g + NR, NG)
    sibling = g + 1 - 2 * core
    east, west = lax.rem(s + 1, NS), lax.rem(s + NS - 1, NS)
    mine = pl.ds(g * MB, MB)

    loads = []
    for i, (src, dst) in enumerate(((ens_hbm, ens), (pert_hbm, pert), (ce_hbm, ce), (cn_hbm, cn),
                                    (cell_hbm, cell_ref), (meas_hbm, meas), (var_hbm, var))):
        loads.append(pltpu.make_async_copy(src, dst, load.at[i]))
    loads[0].start()

    barrier = pltpu.get_barrier_semaphore()
    for n in (east, west):
        pl.semaphore_signal(barrier, inc=1, device_id={"lon": n}, device_id_type=MESH)
    for i in range(1, NG):
        pl.semaphore_signal(barrier, inc=1, device_id={"grp": lax.rem(g + i, NG)}, device_id_type=MESH)
    for c in loads[1:]:
        c.start()

    def remote(src, dst, send, recv, to):
        return pltpu.make_async_remote_copy(
            src_ref=src, dst_ref=dst, send_sem=send, recv_sem=recv, device_id={"grp": to}, device_id_type=MESH)

    def halo(i, c, to):
        rows = pl.ds(c * UNROLL, UNROLL)
        return pltpu.make_async_remote_copy(
            src_ref=hsrc.at[i, rows], dst_ref=hdst.at[i, rows], send_sem=h_send.at[i, c], recv_sem=h_recv.at[i, c],
            device_id={"lon": to}, device_id_type=MESH)

    def pert_copy(to, src):
        half = lax.rem(to, 2)
        return remote(pb.at[lax.rem(to, NR) // 2, half], pt.at[pl.ds(lax.rem(src, NR) * MB, MB)],
                      p_send.at[to], p_recv.at[src], to)

    def z_copy(to, src):
        half = lax.rem(to, 2)
        return remote(zb.at[lax.rem(to, NR) // 2, half], zr.at[pl.ds(src * MB, MB)], z_send.at[to], z_recv.at[src], to)

    def sums_copy(i):
        rows = pl.ds(i * M, M if i == 0 else MR)
        return remote(own_sums.at[rows], other_sums.at[rows], s_send.at[i], s_recv.at[i], sibling)

    def f_copy(to, src):
        return remote(fp.at[to], ft.at[:, pl.ds(src * MB, MB), :], f_send.at[to], f_recv.at[src], to)

    def r_copy(part, to, src):
        x = pl.ds(part * HX, HX)
        return remote(an.at[x, pl.ds(to * MB, MB), :], rb.at[src, x], r_send.at[part, to], r_recv.at[part, src], to)

    def rhs_copy(to_row):
        rows = rhs.at[pl.ds((1 - to_row) * MR + core * (MR // 2), MR // 2)]
        return remote(rows, rows, x_send.at[0], x_recv.at[0], partner)

    def rhs_pass(half):
        rows = rhs.at[pl.ds((1 - row) * MR + half * (MR // 2), MR // 2)]
        return remote(rows, rows, x_send.at[1], x_recv.at[1], sibling)

    def stepped(i, dy, sign):
        k = i // 4
        dx = (1 + 2 * k + k // 2) % 4
        x = lax.rem(my_b + 4 + sign * dx, 4)
        dc = 1 - i % 4 // 2
        return lax.rem(row + dy, 2) * NR + x * 2 + lax.rem(core + dc, 2)

    order = {sign: [stepped(i, 1 - i % 2, sign) for i in range(NG)] for sign in (1, -1)}

    def same_row(body, sign=1):
        for i in range(NR - 1):
            body(order[sign][2 * i + 1])

    def others(body, sign=1, first=0, last=NG - 1):
        for i in range(first, last):
            body(order[sign][i])

    loads[0].wait()
    hsrc[0] = ens[:, :, LON - 1, :]
    hsrc[1] = ens[:, :, 0, :]
    pl.semaphore_wait(barrier, NG - 1 + 2)

    @pl.loop(0, MB // UNROLL)
    def _(c):
        halo(0, c, east).start()
        halo(1, c, west).start()

    for c in loads[1:]:
        c.wait()
    for b in range(NB):
        for h in range(2):
            pb[b, h] = pert[:, b, h * HO:(h + 1) * HO]
    same_row(lambda to: pert_copy(to, g).start())
    pt[pl.ds(lax.rem(g, NR) * MB, MB)] = pb[my_b, core]

    lane = lax.broadcasted_iota(jnp.int32, (LON, LAT), 1)
    sub = lax.broadcasted_iota(jnp.int32, (LON, LAT), 0)
    for l in range(LEV):
        c = ce[l]
        coef[0, l] = 1.0 - c * c
        coef[1, l] = 0.5 * (c * c - c)
        coef[2, l] = 0.5 * (c * c + c)
        c = cn[l]
        coef[3, l] = 1.0 - c * c
        coef[4, l] = jnp.where(lane == LAT - 1, 0.0, 0.5 * (c * c - c))
        coef[5, l] = jnp.where(lane == 0, 0.0, 0.5 * (c * c + c))


    upper = lane >= 64
    odd = (lane // 32) % 2 == 1

    @pl.loop(0, MB // UNROLL)
    def _(c):
        halo(0, c, east).wait()
        halo(1, c, west).wait()
        for q in range(NQ):
            for i in range(UNROLL):
                m = c * UNROLL + i
                tiles = []
                for k in range(4):
                    l = 4 * q + k
                    e = ens[m, l]
                    w_edge = jnp.broadcast_to(hdst[0, m, pl.ds(l, 1), :], (LON, LAT))
                    e_edge = jnp.broadcast_to(hdst[1, m, pl.ds(l, 1), :], (LON, LAT))
                    ww = jnp.where(sub == 0, w_edge, pltpu.roll(e, 1, 0))
                    ee = jnp.where(sub == LON - 1, e_edge, pltpu.roll(e, LON - 1, 0))
                    half = coef[0, l] * e + coef[1, l] * ee + coef[2, l] * ww
                    tiles.append(coef[3, l] * half + coef[4, l] * pltpu.roll(half, LAT - 1, 1)
                                 + coef[5, l] * pltpu.roll(half, 1, 1))
                tiles = swap_blocks(tiles, upper, odd)
                for b in range(NB):
                    for x in range(LON):
                        fp[device_of(b, q), x, pl.ds(m, 1), :] = tiles[b][x:x + 1]

    rows = lax.broadcasted_iota(jnp.int32, (LAT, NO), 0)

    for k in range(NB):
        b = lax.rem(my_b + (1 + 2 * k + k // 2) % 4, NB)
        cell = cell_ref[pl.ds(b, 1), :]
        level = cell // (NS * LON * LAT)
        low = (level % 4) * 32 + cell % 32
        high = (level // 4) * LON + (cell // LAT) % LON
        pick = jnp.where(rows == low, 1.0, 0.0).astype(BF16)
        for o in range(0, NO, 256):
            acc = jnp.zeros((MB, 256), F32)
            hi_o = jnp.broadcast_to(high[:, o:o + 256], (MB, 256))
            pk = pick[:, o:o + 256]
            for q in range(NQ):
                f0, f1 = split2(fp[device_of(b, q)].reshape(LON * MB, LAT))
                t = jnp.dot(jnp.concatenate([f0, f1], axis=1), jnp.concatenate([pk, pk], axis=0),
                            preferred_element_type=F32)
                for x in range(LON):
                    acc = acc + jnp.where(hi_o == q * LON + x, t[x * MB:(x + 1) * MB], 0.0)
            zb[b, o // HO, :, o % HO:o % HO + 256] = acc

        for j in range(NQ):
            if 4 * k + j < NG - 1:
                z_copy(order[1][4 * k + j], g).start()

    zr[mine] = zb[my_b, core]

    same_row(lambda src: pert_copy(g, src).wait_recv(), -1)
    others(lambda src: z_copy(g, src).wait_recv(), -1)
    others(lambda to: f_copy(to, g).start(), last=8)
    ft[:, mine, :] = fp[g]

    eye = jnp.where(lax.broadcasted_iota(jnp.int32, (M, M), 0) == lax.broadcasted_iota(jnp.int32, (M, M), 1), 1.0, 0.0)
    slot = lax.broadcasted_iota(jnp.int32, (1, HO), 1)
    count = count_ref[my_b]
    row_rows = pl.ds(row * MR, MR)

    o = pl.ds(pl.multiple_of(core * HO, HO), HO)
    f = zr[...]
    z = (f - jnp.sum(f, axis=0, keepdims=True) * (1.0 / M)) * SCALE
    zw = z * jnp.where(slot + core * HO < count, 1.0 / var[pl.ds(my_b, 1), o], 0.0)
    own_sums[:M] = dot6(z, zw, ((1,), (1,)))
    sums_copy(0).start()
    d = (meas[pl.ds(my_b, 1), o] + pt[...]) - zr[row_rows]
    own_sums[M:] = dot6(d, zw, ((1,), (1,)))
    sums_copy(1).start()
    sums_copy(0).wait_recv()
    spread = own_sums[:M] + other_sums[:M]
    mat[...] = spread + eye

    low = 1.0 / (jnp.sqrt(jnp.sum(spread * spread)) * 1.0001 + 1.0)
    k = 4.0 / ((1.0 + low) * (1.0 + low))
    inv[...] = (k * low) * ((1.0 + low) * eye - low * mat[...])

    pieces = split3(mat[...])
    for i in range(3):
        mp[:, i * M:(i + 1) * M] = pieces[i]

    def newton(exact, low):
        k = 4.0 / ((1.0 + low) * (1.0 + low))
        m = [mp[:, i * M:(i + 1) * M] for i in range(3)]
        x = split3(inv[...])
        r = (1.0 + low) * eye - (mul(left6(x), right6(m)) if exact else mul(left3(x), right3(m)))
        inv[...] = k * mul(left5(split2(r)), right5(x))
        return k * low

    sums_copy(1).wait_recv()
    rhs[row_rows] = own_sums[M:] + other_sums[M:]
    rhs_copy(1 - row).start()
    others(lambda to: f_copy(to, g).start(), first=8)
    low = lax.fori_loop(0, 7, lambda i, low: newton(False, low), k * low)
    low = lax.fori_loop(0, 3, lambda i, low: newton(True, low), low)
    rhs_copy(row).wait_recv()
    rhs_pass(core).start()
    x = right5(split3(inv[...] * (2.0 / (1.0 + low))))
    rhs_pass(1 - core).wait_recv()
    m = right6([mp[:, i * M:(i + 1) * M] for i in range(3)])
    y = mul(left5(split2(rhs[...])), x)
    for _ in range(2):
        y = y + mul(left5(split2(rhs[...] - mul(left6(split3(y)), m))), x)
    y0, y1 = split2(y * SCALE)
    lhs = jnp.concatenate([y0, y0, y1], axis=1)

    others(lambda src: f_copy(g, src).wait_recv())
    for part in range(2):
        for x in range(part * HX, (part + 1) * HX, 2):
            f = jnp.concatenate([ft[x], ft[x + 1]], axis=1)
            a0, a1 = split2(f - jnp.sum(f, axis=0, keepdims=True) * (1.0 / M))
            u = f + jnp.dot(lhs, jnp.concatenate([a0, a1, a0], axis=0), preferred_element_type=F32)
            an[x] = u[:, :LAT]
            an[x + 1] = u[:, LAT:]
        others(lambda to: r_copy(part, to, g).start())
    own = pltpu.make_async_copy(an.at[:, mine, :], rb.at[g], load.at[0])
    own.start()

    def sent(to):
        z_copy(to, g).wait_send()
        f_copy(to, g).wait_send()

    others(sent)
    same_row(lambda to: pert_copy(to, g).wait_send())
    for i in range(2):
        sums_copy(i).wait_send()
    rhs_copy(1 - row).wait_send()
    rhs_pass(core).wait_send()
    for part in range(2):
        others(lambda src: r_copy(part, g, src).wait_recv())

    for part in range(2):
        others(lambda to: r_copy(part, to, g).wait_send())
    own.wait()


def unpack_kernel(rb, out_hbm, buf, out, loaded, stored):
    lane = lax.broadcasted_iota(jnp.int32, (LON, LAT), 1)
    upper = lane >= 64
    odd = (lane // 32) % 2 == 1

    half = MB // 2

    def load(i):
        q, rows = i // 2, pl.ds(i % 2 * half, half)
        return pltpu.make_async_copy(rb.at[q // 2, :, q % 2, :, rows], buf.at[q, :, :, rows], loaded.at[i])

    def store(i):
        rows, levels = pl.ds(i % 2 * half, half), pl.ds(i // 2 * (LEV // NQ), LEV // NQ)
        return pltpu.make_async_copy(out.at[rows, levels], out_hbm.at[rows, levels], stored.at[i])

    for i in range(2 * NQ):
        load(i).start()
    back = buf.reshape(NQ * NB * LON * MB, LAT)
    for i in range(2 * NQ):
        q = i // 2
        load(i).wait()
        for m in range(i % 2 * half, (i % 2 + 1) * half):
            tiles = swap_blocks([back[pl.ds((q * NB + b) * LON * MB + m, LON, stride=MB), :] for b in range(NB)],
                                upper, odd)
            for k in range(4):
                out[m, 4 * q + k] = tiles[k]
        store(i).start()
    for i in range(2 * NQ):
        store(i).wait()


def on_device(ensemble, courant_east, northward_courant, measured, error_variance, sensor_cell, sensor_count, perturbation):
    dma = pltpu.SemaphoreType.DMA
    vm = lambda *shape: pltpu.VMEM(shape, F32)
    hbm = pl.BlockSpec(memory_space=pltpu.HBM)
    back = pl.pallas_call(
        kernel,
        out_shape=jax.ShapeDtypeStruct((NG, LON, MB, LAT), F32),
        in_specs=[hbm] * 7 + [pl.BlockSpec(memory_space=pltpu.SMEM)],
        out_specs=hbm,
        scratch_shapes=[
            vm(MB, LEV, LON, LAT), vm(LEV, LON, LAT), vm(LEV, LON, LAT), vm(MB, NB, NO),
            pltpu.VMEM((NB, NO), jnp.int32), vm(NB, NO), vm(NB, NO),
            vm(2, MB, LEV, LAT), vm(2, MB, LEV, LAT), vm(6, LEV, LON, LAT),
            vm(NG, LON, MB, LAT), vm(NB, 2, MB, HO), vm(NB, 2, MB, HO),
            vm(M, HO), vm(MR, HO), vm(LON, M, LAT), vm(LON, M, LAT),
            vm(M, M), vm(M, M), vm(M, M), pltpu.VMEM((M, 3 * M), BF16), vm(M + MR, M), vm(M + MR, M),
            dma((7,)), dma((2, MB // UNROLL)), dma((2, MB // UNROLL)),
        ] + [dma((NG,))] * 6 + [dma((2, NG))] * 2 + [dma((2,))] * 4,
        compiler_params=pltpu.CompilerParams(collective_id=0, has_side_effects=True, vmem_limit_bytes=62 << 20),
    )(ensemble, courant_east, northward_courant, perturbation, sensor_cell, measured, error_variance, sensor_count)
    return pl.pallas_call(
        unpack_kernel,
        out_shape=jax.ShapeDtypeStruct((MB, LEV, LON, LAT), F32),
        in_specs=[hbm],
        out_specs=hbm,
        scratch_shapes=[vm(NQ, NB, LON, MB, LAT), vm(MB, LEV, LON, LAT), dma((2 * NQ,)), dma((2 * NQ,))],
        compiler_params=pltpu.CompilerParams(vmem_limit_bytes=62 << 20),
    )(back.reshape(2, NB, 2, LON, MB, LAT))


def solution(mesh):
    return jax.shard_map(
        on_device,
        mesh=mesh,
        in_specs=(
            P("grp", None, "lon", None),
            P(None, "lon", None),
            P(None, "lon", None),
            P("lon", None),
            P("lon", None),
            P("lon", None),
            P("lon"),
            P("grp", "lon", None),
        ),
        out_specs=P("grp", None, "lon", None),
        check_vma=False,
    )
```

```python
import functools
import math

import jax
import jax.numpy as jnp
from jax import lax
from jax.experimental import pallas as pl
from jax.experimental.pallas import tpu as pltpu
from jax.sharding import PartitionSpec as P

MESH = pl.DeviceIdType.MESH
F32 = jnp.float32
BF16 = jnp.bfloat16
NG = 16
NS = 16
MB = 16
M = 256
LEV = 16
LON = 8
LAT = 128
NB = 4
NQ = 4
NO = 1024
HO = NO // 2
HX = LON // 2
SCALE = 1.0 / math.sqrt(M - 1)
UNROLL = 2
NR = NG // 2
MR = NR * MB


def split2(x):
    hi = x.astype(BF16)
    lo = (x - hi.astype(F32)).astype(BF16)
    return hi, lo


def device_of(b, q):
    return (q // 2) * NR + b * 2 + q % 2


def dot6(a, b, dims=((1,), (0,))):
    return lax.dot_general(a, b, (dims, ((), ())), precision=lax.Precision.HIGHEST, preferred_element_type=F32)


def split3(x):
    x0 = x.astype(BF16)
    rest = x - x0.astype(F32)
    x1, x2 = split2(rest)
    return x0, x1, x2


def left3(p):
    return jnp.concatenate([p[0], p[0], p[1]], axis=1)


def right3(p):
    return jnp.concatenate([p[0], p[1], p[0]], axis=0)


def left5(p):
    return jnp.concatenate([p[0], p[0], p[0], p[1], p[1]], axis=1)


def right5(p):
    return jnp.concatenate([p[0], p[1], p[2], p[0], p[1]], axis=0)


def left6(p):
    return jnp.concatenate([p[0], p[0], p[0], p[1], p[1], p[2]], axis=1)


def right6(p):
    return jnp.concatenate([p[0], p[1], p[2], p[0], p[1], p[0]], axis=0)


def mul(a, b):
    return jnp.dot(a, b, preferred_element_type=F32)


def dot3(a, b):
    a0, a1 = split2(a)
    b0, b1 = split2(b)
    return jnp.dot(jnp.concatenate([a0, a0, a1], axis=1), jnp.concatenate([b0, b1, b0], axis=0),
                   preferred_element_type=F32)


def swap_blocks(t, upper, odd):
    u = [None] * 4
    for i in (0, 1):
        u[i] = jnp.where(upper, pltpu.roll(t[i + 2], 64, 1), t[i])
        u[i + 2] = jnp.where(upper, t[i + 2], pltpu.roll(t[i], 64, 1))
    v = [None] * 4
    for i in (0, 2):
        v[i] = jnp.where(odd, pltpu.roll(u[i + 1], 32, 1), u[i])
        v[i + 1] = jnp.where(odd, u[i + 1], pltpu.roll(u[i], 96, 1))
    return v


def kernel(
    ens_hbm, ce_hbm, cn_hbm, pert_hbm, cell_hbm, meas_hbm, var_hbm, count_ref,
    rb,
    ens, ce, cn, pert, cell_ref, meas, var, hsrc, hdst, coef, fp, zb, pb, zr, pt, ft, an, mat, rhs, inv, mp, own_sums, other_sums,
    load, h_send, h_recv, p_send, p_recv, z_send, z_recv,
    f_send, f_recv, r_send, r_recv, x_send, x_recv, s_send, s_recv,
):
    g = lax.axis_index("grp")
    s = lax.axis_index("lon")
    row, my_b, core = g // NR, lax.rem(g, NR) // 2, lax.rem(g, 2)
    partner = lax.rem(g + NR, NG)
    sibling = g + 1 - 2 * core
    east, west = lax.rem(s + 1, NS), lax.rem(s + NS - 1, NS)
    mine = pl.ds(g * MB, MB)

    loads = []
    for i, (src, dst) in enumerate(((ens_hbm, ens), (pert_hbm, pert), (ce_hbm, ce), (cn_hbm, cn),
                                    (cell_hbm, cell_ref), (meas_hbm, meas), (var_hbm, var))):
        loads.append(pltpu.make_async_copy(src, dst, load.at[i]))
    loads[0].start()

    barrier = pltpu.get_barrier_semaphore()
    for n in (east, west):
        pl.semaphore_signal(barrier, inc=1, device_id={"lon": n}, device_id_type=MESH)
    for i in range(1, NG):
        pl.semaphore_signal(barrier, inc=1, device_id={"grp": lax.rem(g + i, NG)}, device_id_type=MESH)
    for c in loads[1:]:
        c.start()

    def remote(src, dst, send, recv, to):
        return pltpu.make_async_remote_copy(
            src_ref=src, dst_ref=dst, send_sem=send, recv_sem=recv, device_id={"grp": to}, device_id_type=MESH)

    def halo(i, c, to):
        rows = pl.ds(c * UNROLL, UNROLL)
        return pltpu.make_async_remote_copy(
            src_ref=hsrc.at[i, rows], dst_ref=hdst.at[i, rows], send_sem=h_send.at[i, c], recv_sem=h_recv.at[i, c],
            device_id={"lon": to}, device_id_type=MESH)

    def pert_copy(to, src):
        half = lax.rem(to, 2)
        return remote(pb.at[lax.rem(to, NR) // 2, half], pt.at[pl.ds(lax.rem(src, NR) * MB, MB)],
                      p_send.at[to], p_recv.at[src], to)

    def z_copy(to, src):
        half = lax.rem(to, 2)
        return remote(zb.at[lax.rem(to, NR) // 2, half], zr.at[pl.ds(src * MB, MB)], z_send.at[to], z_recv.at[src], to)

    def sums_copy(i):
        rows = pl.ds(i * M, M if i == 0 else MR)
        return remote(own_sums.at[rows], other_sums.at[rows], s_send.at[i], s_recv.at[i], sibling)

    def f_copy(to, src):
        return remote(fp.at[to], ft.at[:, pl.ds(src * MB, MB), :], f_send.at[to], f_recv.at[src], to)

    def r_copy(part, to, src):
        x = pl.ds(part * HX, HX)
        return remote(an.at[x, pl.ds(to * MB, MB), :], rb.at[src, x], r_send.at[part, to], r_recv.at[part, src], to)

    def rhs_copy(to_row):
        rows = rhs.at[pl.ds((1 - to_row) * MR + core * (MR // 2), MR // 2)]
        return remote(rows, rows, x_send.at[0], x_recv.at[0], partner)

    def rhs_pass(half):
        rows = rhs.at[pl.ds((1 - row) * MR + half * (MR // 2), MR // 2)]
        return remote(rows, rows, x_send.at[1], x_recv.at[1], sibling)

    def stepped(i, dy, sign):
        k = i // 4
        dx = (1 + 2 * k + k // 2) % 4
        x = lax.rem(my_b + 4 + sign * dx, 4)
        dc = 1 - i % 4 // 2
        return lax.rem(row + dy, 2) * NR + x * 2 + lax.rem(core + dc, 2)

    order = {sign: [stepped(i, 1 - i % 2, sign) for i in range(NG)] for sign in (1, -1)}

    def same_row(body, sign=1):
        for i in range(NR - 1):
            body(order[sign][2 * i + 1])

    def others(body, sign=1, first=0, last=NG - 1):
        for i in range(first, last):
            body(order[sign][i])

    loads[0].wait()
    hsrc[0] = ens[:, :, LON - 1, :]
    hsrc[1] = ens[:, :, 0, :]
    pl.semaphore_wait(barrier, NG - 1 + 2)

    @pl.loop(0, MB // UNROLL)
    def _(c):
        halo(0, c, east).start()
        halo(1, c, west).start()

    for c in loads[1:]:
        c.wait()
    for b in range(NB):
        for h in range(2):
            pb[b, h] = pert[:, b, h * HO:(h + 1) * HO]
    same_row(lambda to: pert_copy(to, g).start())
    pt[pl.ds(lax.rem(g, NR) * MB, MB)] = pb[my_b, core]

    lane = lax.broadcasted_iota(jnp.int32, (LON, LAT), 1)
    sub = lax.broadcasted_iota(jnp.int32, (LON, LAT), 0)
    for l in range(LEV):
        c = ce[l]
        coef[0, l] = 1.0 - c * c
        coef[1, l] = 0.5 * (c * c - c)
        coef[2, l] = 0.5 * (c * c + c)
        c = cn[l]
        coef[3, l] = 1.0 - c * c
        coef[4, l] = jnp.where(lane == LAT - 1, 0.0, 0.5 * (c * c - c))
        coef[5, l] = jnp.where(lane == 0, 0.0, 0.5 * (c * c + c))


    upper = lane >= 64
    odd = (lane // 32) % 2 == 1

    @pl.loop(0, MB // UNROLL)
    def _(c):
        halo(0, c, east).wait()
        halo(1, c, west).wait()
        for q in range(NQ):
            for i in range(UNROLL):
                m = c * UNROLL + i
                tiles = []
                for k in range(4):
                    l = 4 * q + k
                    e = ens[m, l]
                    w_edge = jnp.broadcast_to(hdst[0, m, pl.ds(l, 1), :], (LON, LAT))
                    e_edge = jnp.broadcast_to(hdst[1, m, pl.ds(l, 1), :], (LON, LAT))
                    ww = jnp.where(sub == 0, w_edge, pltpu.roll(e, 1, 0))
                    ee = jnp.where(sub == LON - 1, e_edge, pltpu.roll(e, LON - 1, 0))
                    half = coef[0, l] * e + coef[1, l] * ee + coef[2, l] * ww
                    tiles.append(coef[3, l] * half + coef[4, l] * pltpu.roll(half, LAT - 1, 1)
                                 + coef[5, l] * pltpu.roll(half, 1, 1))
                tiles = swap_blocks(tiles, upper, odd)
                for b in range(NB):
                    for x in range(LON):
                        fp[device_of(b, q), x, pl.ds(m, 1), :] = tiles[b][x:x + 1]

    rows = lax.broadcasted_iota(jnp.int32, (LAT, NO), 0)

    for k in range(NB):
        b = lax.rem(my_b + (1 + 2 * k + k // 2) % 4, NB)
        cell = cell_ref[pl.ds(b, 1), :]
        level = cell // (NS * LON * LAT)
        low = (level % 4) * 32 + cell % 32
        high = (level // 4) * LON + (cell // LAT) % LON
        pick = jnp.where(rows == low, 1.0, 0.0).astype(BF16)
        for o in range(0, NO, 256):
            acc = jnp.zeros((MB, 256), F32)
            hi_o = jnp.broadcast_to(high[:, o:o + 256], (MB, 256))
            pk = pick[:, o:o + 256]
            for q in range(NQ):
                f0, f1 = split2(fp[device_of(b, q)].reshape(LON * MB, LAT))
                t = jnp.dot(jnp.concatenate([f0, f1], axis=1), jnp.concatenate([pk, pk], axis=0),
                            preferred_element_type=F32)
                for x in range(LON):
                    acc = acc + jnp.where(hi_o == q * LON + x, t[x * MB:(x + 1) * MB], 0.0)
            zb[b, o // HO, :, o % HO:o % HO + 256] = acc

        for j in range(NQ):
            if 4 * k + j < NG - 1:
                z_copy(order[1][4 * k + j], g).start()

    zr[mine] = zb[my_b, core]

    others(lambda src: z_copy(g, src).wait_recv(), -1)
    others(lambda to: f_copy(to, g).start(), last=8)
    ft[:, mine, :] = fp[g]

    eye = jnp.where(lax.broadcasted_iota(jnp.int32, (M, M), 0) == lax.broadcasted_iota(jnp.int32, (M, M), 1), 1.0, 0.0)
    slot = lax.broadcasted_iota(jnp.int32, (1, HO), 1)
    count = count_ref[my_b]
    row_rows = pl.ds(row * MR, MR)

    o = pl.ds(pl.multiple_of(core * HO, HO), HO)
    f = zr[...]
    z = (f - jnp.sum(f, axis=0, keepdims=True) * (1.0 / M)) * SCALE
    zw = z * jnp.where(slot + core * HO < count, 1.0 / var[pl.ds(my_b, 1), o], 0.0)
    own_sums[:M] = dot6(z, zw, ((1,), (1,)))
    sums_copy(0).start()
    same_row(lambda src: pert_copy(g, src).wait_recv(), -1)
    d = (meas[pl.ds(my_b, 1), o] + pt[...]) - zr[row_rows]
    own_sums[M:] = dot6(d, zw, ((1,), (1,)))
    sums_copy(1).start()
    sums_copy(0).wait_recv()
    spread = own_sums[:M] + other_sums[:M]
    mat[...] = spread + eye

    low = 1.0 / (jnp.sqrt(jnp.sum(spread * spread)) * 1.0001 + 1.0)
    k = 4.0 / ((1.0 + low) * (1.0 + low))
    inv[...] = (k * low) * ((1.0 + low) * eye - low * mat[...])

    pieces = split3(mat[...])
    for i in range(3):
        mp[:, i * M:(i + 1) * M] = pieces[i]

    def newton(exact, low):
        k = 4.0 / ((1.0 + low) * (1.0 + low))
        m = [mp[:, i * M:(i + 1) * M] for i in range(3)]
        x = split3(inv[...])
        r = (1.0 + low) * eye - (mul(left6(x), right6(m)) if exact else mul(left3(x), right3(m)))
        inv[...] = k * mul(left5(split2(r)), right5(x))
        return k * low

    sums_copy(1).wait_recv()
    rhs[row_rows] = own_sums[M:] + other_sums[M:]
    rhs_copy(1 - row).start()
    others(lambda to: f_copy(to, g).start(), first=8)
    low = lax.fori_loop(0, 7, lambda i, low: newton(False, low), k * low)
    low = lax.fori_loop(0, 3, lambda i, low: newton(True, low), low)
    rhs_copy(row).wait_recv()
    rhs_pass(core).start()
    x = right5(split3(inv[...] * (2.0 / (1.0 + low))))
    rhs_pass(1 - core).wait_recv()
    m = right6([mp[:, i * M:(i + 1) * M] for i in range(3)])
    y = mul(left5(split2(rhs[...])), x)
    for _ in range(2):
        y = y + mul(left5(split2(rhs[...] - mul(left6(split3(y)), m))), x)
    y0, y1 = split2(y * SCALE)
    lhs = jnp.concatenate([y0, y0, y1], axis=1)

    others(lambda src: f_copy(g, src).wait_recv())
    for part in range(2):
        for x in range(part * HX, (part + 1) * HX, 2):
            f = jnp.concatenate([ft[x], ft[x + 1]], axis=1)
            a0, a1 = split2(f - jnp.sum(f, axis=0, keepdims=True) * (1.0 / M))
            u = f + jnp.dot(lhs, jnp.concatenate([a0, a1, a0], axis=0), preferred_element_type=F32)
            an[x] = u[:, :LAT]
            an[x + 1] = u[:, LAT:]
        others(lambda to: r_copy(part, to, g).start())
    own = pltpu.make_async_copy(an.at[:, mine, :], rb.at[g], load.at[0])
    own.start()

    def sent(to):
        z_copy(to, g).wait_send()
        f_copy(to, g).wait_send()

    others(sent)
    same_row(lambda to: pert_copy(to, g).wait_send())
    for i in range(2):
        sums_copy(i).wait_send()
    rhs_copy(1 - row).wait_send()
    rhs_pass(core).wait_send()
    for part in range(2):
        others(lambda src: r_copy(part, g, src).wait_recv())

    for part in range(2):
        others(lambda to: r_copy(part, to, g).wait_send())
    own.wait()


def unpack_kernel(rb, out_hbm, buf, out, loaded, stored):
    lane = lax.broadcasted_iota(jnp.int32, (LON, LAT), 1)
    upper = lane >= 64
    odd = (lane // 32) % 2 == 1

    half = MB // 2

    def load(i):
        q, rows = i // 2, pl.ds(i % 2 * half, half)
        return pltpu.make_async_copy(rb.at[q // 2, :, q % 2, :, rows], buf.at[q, :, :, rows], loaded.at[i])

    def store(i):
        rows, levels = pl.ds(i % 2 * half, half), pl.ds(i // 2 * (LEV // NQ), LEV // NQ)
        return pltpu.make_async_copy(out.at[rows, levels], out_hbm.at[rows, levels], stored.at[i])

    for i in range(2 * NQ):
        load(i).start()
    back = buf.reshape(NQ * NB * LON * MB, LAT)
    for i in range(2 * NQ):
        q = i // 2
        load(i).wait()
        for m in range(i % 2 * half, (i % 2 + 1) * half):
            tiles = swap_blocks([back[pl.ds((q * NB + b) * LON * MB + m, LON, stride=MB), :] for b in range(NB)],
                                upper, odd)
            for k in range(4):
                out[m, 4 * q + k] = tiles[k]
        store(i).start()
    for i in range(2 * NQ):
        store(i).wait()


def on_device(ensemble, courant_east, northward_courant, measured, error_variance, sensor_cell, sensor_count, perturbation):
    dma = pltpu.SemaphoreType.DMA
    vm = lambda *shape: pltpu.VMEM(shape, F32)
    hbm = pl.BlockSpec(memory_space=pltpu.HBM)
    back = pl.pallas_call(
        kernel,
        out_shape=jax.ShapeDtypeStruct((NG, LON, MB, LAT), F32),
        in_specs=[hbm] * 7 + [pl.BlockSpec(memory_space=pltpu.SMEM)],
        out_specs=hbm,
        scratch_shapes=[
            vm(MB, LEV, LON, LAT), vm(LEV, LON, LAT), vm(LEV, LON, LAT), vm(MB, NB, NO),
            pltpu.VMEM((NB, NO), jnp.int32), vm(NB, NO), vm(NB, NO),
            vm(2, MB, LEV, LAT), vm(2, MB, LEV, LAT), vm(6, LEV, LON, LAT),
            vm(NG, LON, MB, LAT), vm(NB, 2, MB, HO), vm(NB, 2, MB, HO),
            vm(M, HO), vm(MR, HO), vm(LON, M, LAT), vm(LON, M, LAT),
            vm(M, M), vm(M, M), vm(M, M), pltpu.VMEM((M, 3 * M), BF16), vm(M + MR, M), vm(M + MR, M),
            dma((7,)), dma((2, MB // UNROLL)), dma((2, MB // UNROLL)),
        ] + [dma((NG,))] * 6 + [dma((2, NG))] * 2 + [dma((2,))] * 4,
        compiler_params=pltpu.CompilerParams(collective_id=0, has_side_effects=True, vmem_limit_bytes=62 << 20),
    )(ensemble, courant_east, northward_courant, perturbation, sensor_cell, measured, error_variance, sensor_count)
    return pl.pallas_call(
        unpack_kernel,
        out_shape=jax.ShapeDtypeStruct((MB, LEV, LON, LAT), F32),
        in_specs=[hbm],
        out_specs=hbm,
        scratch_shapes=[vm(NQ, NB, LON, MB, LAT), vm(MB, LEV, LON, LAT), dma((2 * NQ,)), dma((2 * NQ,))],
        compiler_params=pltpu.CompilerParams(vmem_limit_bytes=62 << 20),
    )(back.reshape(2, NB, 2, LON, MB, LAT))


def solution(mesh):
    return jax.shard_map(
        on_device,
        mesh=mesh,
        in_specs=(
            P("grp", None, "lon", None),
            P(None, "lon", None),
            P(None, "lon", None),
            P("lon", None),
            P("lon", None),
            P("lon", None),
            P("lon"),
            P("grp", "lon", None),
        ),
        out_specs=P("grp", None, "lon", None),
        check_vma=False,
    )
```
